256 devices in a mesh: gx: 32 (over x, z_hi, core), gy: 8 (over y, z_lo).
Axes of the slice: x: 4, y: 4, z: 8 (z_hi: 4, z_lo: 2; z = z_hi * 2 + z_lo), core: 2. Of those that a mesh axis runs over, the one named last changes fastest.
Arguments:
- flow_state: float32 [5, 2, 512, 4096], P(None, None, 'gx', 'gy'), may hold values from -1 to 5, as said below
- colour_map: int32 [2, 512, 4096], P(None, 'gx', 'gy'), may hold values from 0 to 26
- cell_flags: int32 [512, 4096], P('gx', 'gy'), may hold values 0 or 1
- probe_weights: float32 [2, 27, 5], replicated, may hold values from -6 to 6
Outputs:
- tangent_residual: float32 [2, 5, 2, 512, 4096], P(None, None, None, 'gx', 'gy')
The draws below stay inside these ranges and needn't reach their ends.
Inputs may be any that keep to these rules, and one draw needn't show every extreme that they name: `flow_state`: density lies in 0.7 to 1.3 and pressure, computed as in the reference program, in 0.6 to 1.4 at every cell.
All inputs are finite; a program needn't handle non-finite values. No bound on the sum of `cell_flags` on one device may be relied on, other than what follows from the above.
Results may differ from the reference program's by a relative error of at most 0.0003.
Values sent between devices are 32-bit elements; how exact they have to be, the bound alone decides.
No kernel may reach another device: no remote copies, remote signals or barrier semaphores. Data moves between devices by JAX's collectives and lax.ppermute only.
A program may use at most 64 MiB of HBM per device.

```python
import jax
import jax.numpy as jnp
from jax import lax

VARIABLES = 5
PROBES = 2
COLOURS = 27
LEVELS = 2
CX = 16
NX = 512
NY = 4096


HEAT_RATIO = 1.4


def draw_flow_state(key, part):
    key = jax.random.fold_in(key, 11)
    subkeys = jax.random.split(key, 3)
    grid_shape = (LEVELS, NX, NY)
    specific_weight_per_volume = jax.random.uniform(subkeys[0], grid_shape, jnp.float32, minval=0.7, maxval=1.3)
    fluid_motion_vector = jax.random.uniform(subkeys[1], (3,) + grid_shape, jnp.float32, minval=-0.5, maxval=0.5)
    normal_stress_scalar = jax.random.uniform(subkeys[2], grid_shape, jnp.float32, minval=0.6, maxval=1.4)
    momentum = specific_weight_per_volume * fluid_motion_vector
    energy = normal_stress_scalar / (HEAT_RATIO - 1.0) + 0.5 * specific_weight_per_volume * jnp.sum(fluid_motion_vector * fluid_motion_vector, axis=0)
    return jnp.concatenate([specific_weight_per_volume[None], momentum, energy[None]], axis=0)


def set_ends(result, key, low, top_value):
    longest = result.shape.index(max(result.shape))
    spots = []
    for shift in (0, 1):
        where = [jax.random.randint(jax.random.fold_in(key, axis), (), 0, length) for axis, length in enumerate(result.shape)]
        where[longest] = (where[longest] + shift) % result.shape[longest]
        spots.append(tuple(where))
    return result.at[spots[0]].set(low).at[spots[1]].set(top_value)


def normal_values(key, shape, deviation, limit, held_as=jnp.bfloat16):
    values = jax.random.normal(key, shape, jnp.float32) * deviation
    return jnp.minimum(jnp.maximum(values, -limit), limit).astype(held_as)


def setup_inputs(seed: int = 0) -> dict:
    key_of = jax.random.split(jax.random.key(seed), 5)
    return {
        "flow_state": draw_flow_state(jax.random.fold_in(key_of[4], 71), 0),
        "colour_map": set_ends(jax.random.randint(key_of[1], (LEVELS, NX, NY), 0, COLOURS), jax.random.fold_in(key_of[1], 1), 0, COLOURS - 1).astype(jnp.int32),
        "cell_flags": set_ends((jax.random.randint(key_of[2], (NX, NY), 0, 8) < 1).astype(jnp.int32), jax.random.fold_in(key_of[2], 1), 0, 1),
        "probe_weights": normal_values(key_of[3], (PROBES, COLOURS, VARIABLES), 1.0, 6.0, jnp.float32),
    }


GAMMA = 1.4
VISCOSITY = 0.2
CONDUCT = 0.2 * 1.4 / (0.4 * 0.72)
DISSIPATE = 0.5

def pair_list(facing):
    chosen = []
    for entry_pair in [(0, facing), (1, facing), (2, facing), (facing, 0), (facing, 1), (facing, 2), (0, 0), (1, 1), (2, 2), (3, facing)]:
        if entry_pair not in chosen:
            chosen.append(entry_pair)
    return chosen

def trim_axis(values, start, trim, from_end):
    axis_number = values.ndim - from_end
    return lax.slice_in_dim(values, start, values.shape[axis_number] - trim, axis=axis_number)

def basic_unknowns(grid_tensor_list):
    specific_weight_per_volume = grid_tensor_list[0]
    fluid_motion_vector = grid_tensor_list[1:4] / specific_weight_per_volume
    kinetic = 0.5 * lax.optimization_barrier(jnp.sum(grid_tensor_list[1:4] * fluid_motion_vector, axis=0))
    normal_stress_scalar = (GAMMA - 1.0) * (grid_tensor_list[4] - kinetic)
    thermal_level = normal_stress_scalar / specific_weight_per_volume
    return (specific_weight_per_volume, fluid_motion_vector, normal_stress_scalar, thermal_level)

def level_grad(grid_tensor_list):
    levels = grid_tensor_list.shape[-3]
    level_above = jnp.concatenate([grid_tensor_list[..., 1:, :, :], grid_tensor_list[..., -1:, :, :]], axis=-3)
    level_below = jnp.concatenate([grid_tensor_list[..., :1, :, :], grid_tensor_list[..., :-1, :, :]], axis=-3)
    position = jnp.arange(levels)
    factor = jnp.where((position == 0) | (position == levels - 1), 1.0, 0.5).astype(grid_tensor_list.dtype)
    return (level_above - level_below) * factor[:, None, None]

def gradients(extended_solution):
    specific_weight_per_volume, fluid_motion_vector, normal_stress_scalar, thermal_level = basic_unknowns(extended_solution)
    physical_measure = jnp.concatenate([fluid_motion_vector, thermal_level[None]], axis=0)
    along_x = 0.5 * (physical_measure[:, :, 2:, 1:-1] - physical_measure[:, :, :-2, 1:-1])
    along_y = 0.5 * (physical_measure[:, :, 1:-1, 2:] - physical_measure[:, :, 1:-1, :-2])
    along_z = level_grad(physical_measure)[:, :, 1:-1, 1:-1]
    return jnp.stack([along_x, along_y, along_z], axis=1)

def pick_components(gradient_set, facing):
    return jnp.stack([gradient_set[entry_pair[0], entry_pair[1]] for entry_pair in pair_list(facing)])

def viscous_face(facing, comps_low, comps_high, vel_low, vel_high):
    chosen = pair_list(facing)

    def face_grad(variable, towards):
        position = chosen.index((variable, towards))
        return 0.5 * (comps_low[position] + comps_high[position])
    vel_face = 0.5 * (vel_low + vel_high)
    diverge = face_grad(0, 0) + face_grad(1, 1) + face_grad(2, 2)
    stresses = []
    for component in range(3):
        stress_term = VISCOSITY * (face_grad(component, facing) + face_grad(facing, component))
        if component == facing:
            stress_term = stress_term - 2.0 / 3.0 * VISCOSITY * diverge
        stresses.append(stress_term)
    energy = vel_face[0] * stresses[0] + vel_face[1] * stresses[1] + vel_face[2] * stresses[2]
    energy = energy + CONDUCT * face_grad(3, facing)
    return jnp.stack([jnp.zeros_like(energy), stresses[0], stresses[1], stresses[2], energy])

def inviscid_flux(grid_tensor_list, facing):
    specific_weight_per_volume, fluid_motion_vector, normal_stress_scalar, thermal_level = basic_unknowns(grid_tensor_list)
    normal_vel = fluid_motion_vector[facing]
    momenta = []
    for component in range(3):
        momentum_flux = grid_tensor_list[1 + component] * normal_vel
        if component == facing:
            momentum_flux = momentum_flux + normal_stress_scalar
        momenta.append(momentum_flux)
    fluxes = jnp.stack([grid_tensor_list[1 + facing], momenta[0], momenta[1], momenta[2], (grid_tensor_list[4] + normal_stress_scalar) * normal_vel])
    speeds = jnp.sqrt(normal_vel * normal_vel + GAMMA * normal_stress_scalar / specific_weight_per_volume)
    return (fluxes, speeds, fluid_motion_vector)

def direction_divergence(strip, comps, facing):
    from_end = 2 if facing == 0 else 1
    fluxes, speeds, fluid_motion_vector = inviscid_flux(strip, facing)
    central = (7.0 * (trim_axis(fluxes, 1, 2, from_end) + trim_axis(fluxes, 2, 1, from_end)) - (trim_axis(fluxes, 0, 3, from_end) + trim_axis(fluxes, 3, 0, from_end))) / 12.0
    state_jump = trim_axis(strip, 2, 1, from_end) - trim_axis(strip, 1, 2, from_end)
    central = central - DISSIPATE * 0.5 * (trim_axis(speeds, 1, 2, from_end) + trim_axis(speeds, 2, 1, from_end)) * state_jump
    viscous = viscous_face(facing, trim_axis(comps, 0, 1, from_end), trim_axis(comps, 1, 0, from_end), trim_axis(fluid_motion_vector, 1, 2, from_end), trim_axis(fluid_motion_vector, 2, 1, from_end))
    face_sum = central - viscous
    return trim_axis(face_sum, 1, 0, from_end) - trim_axis(face_sum, 0, 1, from_end)

def level_divergence(inner_state, gradient_set):
    fluxes, speeds, fluid_motion_vector = inviscid_flux(inner_state, 2)
    central = 0.5 * (fluxes[:, :-1] + fluxes[:, 1:])
    central = central - DISSIPATE * 0.5 * (speeds[:-1] + speeds[1:]) * (inner_state[:, 1:] - inner_state[:, :-1])
    comps = pick_components(gradient_set, 2)
    viscous = viscous_face(2, comps[:, :-1], comps[:, 1:], fluid_motion_vector[:, :-1], fluid_motion_vector[:, 1:])
    face_sum = central - viscous
    wall_zero = jnp.zeros_like(face_sum[:, :1])
    padded_faces = jnp.concatenate([wall_zero, face_sum, wall_zero], axis=1)
    return padded_faces[:, 1:] - padded_faces[:, :-1]

def assemble(extended_solution, comps_x, comps_y, gradient_set):
    strip_x = extended_solution[:, :, :, 2:-2]
    strip_y = extended_solution[:, :, 2:-2, :]
    inner_state = extended_solution[:, :, 2:-2, 2:-2]
    return -(direction_divergence(strip_x, comps_x, 0) + direction_divergence(strip_y, comps_y, 1) + level_divergence(inner_state, gradient_set))

def compute_all(extended_solution):
    gradient_set = gradients(extended_solution)
    comps_x = pick_components(gradient_set, 0)[:, :, :, 1:-1]
    comps_y = pick_components(gradient_set, 1)[:, :, 1:-1, :]
    return assemble(extended_solution, comps_x, comps_y, gradient_set[:, :, :, 1:-1, 1:-1])

def make_seeds(tinted, probe_weights):
    palette = jnp.arange(probe_weights.shape[1], dtype=jnp.int32)
    onehot = (tinted[None] == palette[:, None, None, None]).astype(probe_weights.dtype)
    return jnp.einsum('pcv,clxy->pvlxy', probe_weights, onehot, precision=lax.Precision.HIGHEST)

def probe_tangents(extended_solution, seed_field):

    def one_probe(probe_seed):
        return jax.jvp(compute_all, (extended_solution,), (probe_seed,))
    primal_out, tangent_out = jax.vmap(one_probe, out_axes=(None, 0))(seed_field)
    return tangent_out

def apply_solid(tangents, seed_inner, solid_flags):
    solid_mask = (solid_flags == 1)[None, None, None]
    return jnp.where(solid_mask, -seed_inner, tangents)

def reference(flow_state, colour_map, cell_flags, probe_weights):
    wrapped = jnp.pad(flow_state, ((0, 0), (0, 0), (2, 2), (2, 2)), mode='wrap')
    colour_pad = jnp.pad(colour_map, ((0, 0), (2, 2), (2, 2)), mode='wrap')
    block_count = NX // CX

    def one_block(block_index):
        row_start = (block_index * CX).astype(jnp.int32)
        extended_solution = lax.dynamic_slice_in_dim(wrapped, row_start, CX + 4, axis=2)
        tinted = lax.dynamic_slice_in_dim(colour_pad, row_start, CX + 4, axis=1)
        seed_field = make_seeds(tinted, probe_weights)
        tangents = probe_tangents(extended_solution, seed_field)
        solid_flags = lax.dynamic_slice_in_dim(cell_flags, row_start, CX, axis=0)
        return apply_solid(tangents, seed_field[:, :, :, 2:-2, 2:-2], solid_flags)
    block_results = lax.map(one_block, jnp.arange(block_count, dtype=jnp.int32))
    moved = jnp.moveaxis(block_results, 0, 3)
    return moved.reshape((PROBES, VARIABLES, LEVELS, NX, NY))
```

```python
import functools

import jax
import jax.numpy as jnp
from jax import lax
from jax.experimental import pallas as pl
from jax.experimental.pallas import tpu as pltpu
from jax.sharding import PartitionSpec as P

MU = 0.2
KAPPA = 0.2 * 1.4 / (0.4 * 0.72)
BASE = 12
ROWS = 40


def pack_x(flow, colour, to_near, to_far):
    odd = lax.rem(lax.axis_index("gx"), 2)

    def fill(dst, start):
        for l in range(2):
            for v in range(5):
                dst[4 * v + 2 * l : 4 * v + 2 * l + 2, :] = flow[v, l, start : start + 2, :]
            dst[20 + 2 * l : 22 + 2 * l, :] = colour[l, start : start + 2, :].astype(jnp.float32)

    @pl.when(odd == 0)
    def _():
        fill(to_near, 14)
        fill(to_far, 0)

    @pl.when(odd == 1)
    def _():
        fill(to_near, 0)
        fill(to_far, 14)


def pack_y(flow, colour, from_near, from_far, ext, to_near, to_far):
    odd_x = lax.rem(lax.axis_index("gx"), 2)
    odd_y = lax.rem(lax.axis_index("gy"), 2)
    for l in range(2):
        for c in range(4):
            lanes = slice(128 * c, 128 * c + 128)
            for v in range(5):
                ext[v, l, c, BASE : BASE + 16, :] = flow[v, l, :, lanes]
            ext[5, l, c, BASE : BASE + 16, :] = colour[l, :, lanes].astype(jnp.float32)

    def halo(src, row):
        for l in range(2):
            for v in range(6):
                for c in range(4):
                    ext[v, l, c, row : row + 2, :] = src[4 * v + 2 * l : 4 * v + 2 * l + 2, 128 * c : 128 * c + 128]

    @pl.when(odd_x == 0)
    def _():
        halo(from_far, BASE - 2)
        halo(from_near, BASE + 16)

    @pl.when(odd_x == 1)
    def _():
        halo(from_near, BASE - 2)
        halo(from_far, BASE + 16)

    lane = lax.broadcasted_iota(jnp.int32, (24, 128), 1)

    def edge(c, first):
        made = jnp.zeros((24, 128), jnp.float32)
        for l in range(2):
            for v in range(6):
                at = 2 * (6 * l + v)
                cells = ext[v, l, c, BASE - 4 : BASE + 20, :]
                moved = pltpu.roll(cells, (at - first) % 128, 1)
                made = jnp.where((lane >= at) & (lane < at + 2), moved, made)
        return made

    left, right = edge(0, 0), edge(3, 126)

    @pl.when(odd_y == 0)
    def _():
        to_near[...] = right
        to_far[...] = left

    @pl.when(odd_y == 1)
    def _():
        to_near[...] = left
        to_far[...] = right


def tangent(ext, from_near, from_far, flags, table, out, rim, seeds, prim, speed, flux, stress, face):
    odd_y = lax.rem(lax.axis_index("gy"), 2)
    lane = lax.broadcasted_iota(jnp.int32, (24, 128), 1)

    def unpack(low, high):
        for l in range(2):
            for v in range(6):
                at = 2 * (6 * l + v)
                rim[v, l, BASE - 4 : BASE + 20, :] = jnp.where(
                    lane < 64,
                    pltpu.roll(high[...], (-at) % 128, 1),
                    pltpu.roll(low[...], (126 - at) % 128, 1),
                )

    @pl.when(odd_y == 0)
    def _():
        unpack(from_far, from_near)

    @pl.when(odd_y == 1)
    def _():
        unpack(from_near, from_far)

    def state(v, l, row, tiles=5):
        parts = [ext[v, l, c, row : row + 8, :] for c in range(4)]
        if tiles == 5:
            parts.append(rim[v, l, row : row + 8, :])
        return jnp.concatenate(parts, axis=1)

    def get(ref, f, l, row, tiles=5):
        return jnp.concatenate([ref[f, l, c, row : row + 8, :] for c in range(tiles)], axis=1)

    def put(ref, f, l, row, value):
        for c in range(value.shape[1] // 128):
            ref[f, l, c, row : row + 8, :] = value[:, 128 * c : 128 * c + 128]

    def ahead(value, step=1):
        return pltpu.roll(value, (-step) % value.shape[1], 1)

    for l in range(2):
        for row in (8, 16, 24):
            for c in range(5):
                if c < 4:
                    u5 = [ext[v, l, c, row : row + 8, :] for v in range(6)]
                else:
                    u5 = [rim[v, l, row : row + 8, :] for v in range(6)]
                shade = u5[5].astype(jnp.int32) & 127
                r = 1.0 / u5[0]
                vel = [u5[1 + e] * r for e in range(3)]
                half = 0.5 * (vel[0] * vel[0] + vel[1] * vel[1] + vel[2] * vel[2])
                pressure = 0.4 * (u5[4] - half * u5[0])
                heat = pressure * r
                total = u5[4] + pressure
                for e in range(3):
                    prim[e, l, c, row : row + 8, :] = vel[e]
                prim[3, l, c, row : row + 8, :] = heat
                inverse = []
                for e in range(3):
                    square = vel[e] * vel[e] + 1.4 * heat
                    inv = lax.rsqrt(square)
                    speed[3 * e, l, c, row : row + 8, :] = 0.25 * (square * inv)
                    inverse.append(0.25 * inv)
                for p in range(2):
                    d = []
                    for v in range(5):
                        row_of = jnp.broadcast_to(table[5 * p + v : 5 * p + v + 1, :], (8, 128))
                        d.append(jnp.take_along_axis(row_of, shade, axis=1, mode="promise_in_bounds"))
                        seeds[5 * p + v, l, c, row : row + 8, :] = d[v]
                    dvel = [(d[1 + e] - vel[e] * d[0]) * r for e in range(3)]
                    dpress = 0.4 * (d[4] - (vel[0] * d[1] + vel[1] * d[2] + vel[2] * d[3]) + half * d[0])
                    dheat = (dpress - heat * d[0]) * r
                    for e in range(3):
                        prim[4 + 4 * p + e, l, c, row : row + 8, :] = dvel[e]
                    prim[7 + 4 * p, l, c, row : row + 8, :] = dheat
                    warm = 0.7 * dheat
                    dtotal = d[4] + dpress
                    for e in range(3):
                        speed[3 * e + 1 + p, l, c, row : row + 8, :] = (vel[e] * dvel[e] + warm) * inverse[e]
                        for g in range(3):
                            move = d[1 + g] * vel[e] + u5[1 + g] * dvel[e]
                            if g == e:
                                move = move + dpress
                            flux[8 * e + 4 * p + g, l, c, row : row + 8, :] = move
                        flux[8 * e + 4 * p + 3, l, c, row : row + 8, :] = dtotal * vel[e] + total * dvel[e]

    quarter = 0.25 * MU
    for row in (8, 16, 24):
        for k in range(3):
            grad_z = [2.0 * (get(prim, 4 * k + q, 1, row) - get(prim, 4 * k + q, 0, row)) for q in range(4)]
            for l in range(2):
                here = [get(prim, 4 * k + q, l, row) for q in range(4)]
                grad_x = [get(prim, 4 * k + q, l, row + 1) - get(prim, 4 * k + q, l, row - 1) for q in range(4)]
                grad_y = [ahead(h, 1) - ahead(h, -1) for h in here]
                third = (2.0 / 3.0) * (grad_x[0] + grad_y[1] + grad_z[2])
                base = 0 if k == 0 else 6 + 9 * (k - 1)
                put(stress, base, l, row, quarter * (2.0 * grad_x[0] - third))
                put(stress, base + 1, l, row, quarter * (grad_y[0] + grad_x[1]))
                put(stress, base + 2, l, row, quarter * (grad_z[0] + grad_x[2]))
                put(stress, base + 3, l, row, quarter * (2.0 * grad_y[1] - third))
                put(stress, base + 4, l, row, quarter * (grad_z[1] + grad_y[2]))
                put(stress, base + 5, l, row, quarter * (2.0 * grad_z[2] - third))
                if k > 0:
                    put(stress, base + 6, l, row, (0.25 * KAPPA) * grad_x[3])
                    put(stress, base + 7, l, row, (0.25 * KAPPA) * grad_y[3])
                    put(stress, base + 8, l, row, (0.25 * KAPPA) * grad_z[3])

    parts_of = ((0, 1, 2), (1, 3, 4), (2, 4, 5))

    for l in range(2):
        for row in (8, 16, 24):
            jump = [state(v, l, row + 1, 4) - state(v, l, row, 4) for v in range(5)]
            s_sum = get(speed, 0, l, row, 4) + get(speed, 0, l, row + 1, 4)
            v_sum = [0.5 * (get(prim, e, l, row, 4) + get(prim, e, l, row + 1, 4)) for e in range(3)]
            t_sum = [get(stress, t, l, row, 4) + get(stress, t, l, row + 1, 4) for t in parts_of[0]]
            for p in range(2):
                ds = get(speed, 1 + p, l, row, 4) + get(speed, 1 + p, l, row + 1, 4)
                for v in range(5):
                    djump = get(seeds, 5 * p + v, l, row + 1, 4) - get(seeds, 5 * p + v, l, row, 4)
                    made = ds * jump[v] + s_sum * djump
                    if v == 4:
                        for e in range(3):
                            f = 6 + 9 * p + parts_of[0][e]
                            dt = get(stress, f, l, row, 4) + get(stress, f, l, row + 1, 4)
                            dv = 0.5 * (get(prim, 4 + 4 * p + e, l, row, 4) + get(prim, 4 + 4 * p + e, l, row + 1, 4))
                            made = made + v_sum[e] * dt + dv * t_sum[e]
                    put(face, 5 * p + v, l, row, made)

    for t in range(2):
        row = BASE + 8 * t
        solid = flags[8 * t : 8 * t + 8, :] == 1
        jump_z = [state(v, 1, row, 4) - state(v, 0, row, 4) for v in range(5)]
        s_z = get(speed, 6, 0, row, 4) + get(speed, 6, 1, row, 4)
        v_z = [0.5 * (get(prim, e, 0, row, 4) + get(prim, e, 1, row, 4)) for e in range(3)]
        t_z = [get(stress, i, 0, row, 4) + get(stress, i, 1, row, 4) for i in parts_of[2]]
        through = []
        for p in range(2):
            ds = get(speed, 7 + p, 0, row, 4) + get(speed, 7 + p, 1, row, 4)
            for v in range(5):
                seed0, seed1 = get(seeds, 5 * p + v, 0, row, 4), get(seeds, 5 * p + v, 1, row, 4)
                if v == 0:
                    mean = get(seeds, 5 * p + 3, 0, row, 4) + get(seeds, 5 * p + 3, 1, row, 4)
                else:
                    f = 16 + 4 * p + v - 1
                    mean = get(flux, f, 0, row, 4) + get(flux, f, 1, row, 4)
                made = 0.5 * mean - (ds * jump_z[v] + s_z * (seed1 - seed0))
                if 1 <= v <= 3:
                    f = 6 + 9 * p + parts_of[2][v - 1]
                    made = made - (get(stress, f, 0, row, 4) + get(stress, f, 1, row, 4))
                if v == 4:
                    work = get(stress, 6 + 9 * p + 8, 0, row, 4) + get(stress, 6 + 9 * p + 8, 1, row, 4)
                    for e in range(3):
                        f = 6 + 9 * p + parts_of[2][e]
                        dt = get(stress, f, 0, row, 4) + get(stress, f, 1, row, 4)
                        dv = 0.5 * (get(prim, 4 + 4 * p + e, 0, row, 4) + get(prim, 4 + 4 * p + e, 1, row, 4))
                        work = work + v_z[e] * dt + dv * t_z[e]
                    made = made - work
                through.append(made)
        for l in range(2):
            jump, v_sum, t_sum = [], [], []
            for v in range(5):
                here = state(v, l, row)
                jump.append(ahead(here) - here)
            for e in range(3):
                here = get(prim, e, l, row)
                v_sum.append(0.5 * (here + ahead(here)))
                here = get(stress, parts_of[1][e], l, row)
                t_sum.append(here + ahead(here))
            here = get(speed, 3, l, row)
            s_sum = here + ahead(here)
            for p in range(2):
                here = get(speed, 4 + p, l, row)
                ds = here + ahead(here)
                for v in range(5):
                    here = get(seeds, 5 * p + v, l, row)
                    made = ds * jump[v] + s_sum * (ahead(here) - here)
                    if v == 4:
                        for e in range(3):
                            here = get(stress, 6 + 9 * p + parts_of[1][e], l, row)
                            dt = here + ahead(here)
                            here = get(prim, 4 + 4 * p + e, l, row)
                            dv = 0.5 * (here + ahead(here))
                            made = made + v_sum[e] * dt + dv * t_sum[e]
                    if v == 0:
                        cell = get(seeds, 5 * p + 2, l, row)
                    else:
                        cell = get(flux, 8 + 4 * p + v - 1, l, row)
                    third = (1.0 / 12.0) * cell
                    cell = (8.0 / 12.0) * cell - ahead(third, 1) - ahead(third, -1)
                    if v > 0:
                        f = 7 if v == 4 else parts_of[1][v - 1]
                        cell = cell - get(stress, 6 + 9 * p + f, l, row)
                    made = made - cell - ahead(cell)
                    total = (made - ahead(made, -1))[:, :512]
                    if v == 0:
                        at = lambda s: get(seeds, 5 * p + 1, l, row + s, 4)
                    else:
                        at = lambda s: get(flux, 4 * p + v - 1, l, row + s, 4)
                    total = total - (8.0 / 12.0) * (at(1) - at(-1)) + (1.0 / 12.0) * (at(2) - at(-2))
                    if v > 0:
                        f = 6 + 9 * p + (6 if v == 4 else parts_of[0][v - 1])
                        total = total + get(stress, f, l, row + 1, 4) - get(stress, f, l, row - 1, 4)
                    total = total + get(face, 5 * p + v, l, row, 4) - get(face, 5 * p + v, l, row - 1, 4)
                    wall = through[5 * p + v]
                    total = total - wall if l == 0 else total + wall
                    seed = get(seeds, 5 * p + v, l, row, 4)
                    out[p, v, l, 8 * t : 8 * t + 8, :] = jnp.where(solid, -seed, total)


def swap(value, axis, offset):
    count = lax.axis_size(axis)
    pairs = []
    for k in range(0, count, 2):
        i, j = (k + offset) % count, (k + offset + 1) % count
        pairs += [(i, j), (j, i)]
    return lax.ppermute(value, axis, pairs)


def local(flow_state, colour_map, cell_flags, probe_weights):
    f32 = jnp.float32
    vmem = pl.BlockSpec(memory_space=pltpu.VMEM)
    params = pltpu.CompilerParams(vmem_limit_bytes=48 * 1024 * 1024)

    def call(kernel, shapes, n_in, scratch=()):
        return pl.pallas_call(
            kernel,
            out_shape=[jax.ShapeDtypeStruct(s, f32) for s in shapes],
            in_specs=[vmem] * n_in,
            out_specs=[vmem] * len(shapes),
            scratch_shapes=[pltpu.VMEM(s, f32) for s in scratch],
            compiler_params=params,
        )

    table = jnp.pad(jnp.transpose(probe_weights, (0, 2, 1)).reshape(10, 27), ((0, 6), (0, 101)))
    x_near, x_far = call(pack_x, [(24, 512)] * 2, 2)(flow_state, colour_map)
    x_far = swap(x_far, "gx", 1)
    x_near = swap(x_near, "gx", 0)
    ext, y_near, y_far = call(pack_y, [(6, 2, 4, ROWS, 128), (24, 128), (24, 128)], 4)(
        flow_state, colour_map, x_near, x_far
    )
    y_far = swap(y_far, "gy", 1)
    y_near = swap(y_near, "gy", 0)
    fields = lambda n: (n, 2, 5, ROWS, 128)
    (out,) = call(
        tangent,
        [(2, 5, 2, 16, 512)],
        5,
        [(6, 2, ROWS, 128), fields(10), fields(12), fields(9), fields(24), fields(24), (10, 2, 4, ROWS, 128)],
    )(ext, y_near, y_far, cell_flags, table)
    return out


def solution(mesh):
    return jax.shard_map(
        local,
        mesh=mesh,
        in_specs=(P(None, None, "gx", "gy"), P(None, "gx", "gy"), P("gx", "gy"), P()),
        out_specs=P(None, None, None, "gx", "gy"),
        check_vma=False,
    )
```

```python
import jax
import jax.numpy as jnp
from jax import lax
from jax.experimental import pallas as pl
from jax.experimental.pallas import tpu as pltpu
from jax.sharding import PartitionSpec as P

MU = 0.2
KAPPA = 0.2 * 1.4 / (0.4 * 0.72)
BASE = 12
ROWS = 40
STATE, SEED, PRIM, SPEED, FLUX, FIELDS = 0, 6, 16, 28, 31, 39
TENSOR = ((0, 1, 2), (1, 3, 4), (2, 4, 5))


def get(ref, f, l, row):
    tiles = [ref[f, l, c, row : row + 8, :] for c in range(ref.shape[2])]
    return tiles[0] if len(tiles) == 1 else jnp.concatenate(tiles, axis=1)


def put(ref, f, l, row, value):
    for c in range(ref.shape[2]):
        ref[f, l, c, row : row + 8, :] = value[:, 128 * c : 128 * c + 128]


def ahead(value, step=1):
    return pltpu.roll(value, (-step) % value.shape[1], 1)


def pointwise(bank, table, rows, speed_yz=None, flux_yz=None):
    for l in range(2):
        for row in rows:
            for c in range(bank.shape[2]):
                at = (l, c, slice(row, row + 8), slice(None))
                u = [bank[(STATE + v,) + at] for v in range(5)]
                shade = bank[(STATE + 5,) + at].astype(jnp.int32) & 127
                r = 1.0 / u[0]
                vel = [u[1 + e] * r for e in range(3)]
                half = 0.5 * (vel[0] * vel[0] + vel[1] * vel[1] + vel[2] * vel[2])
                pressure = 0.4 * (u[4] - half * u[0])
                heat = pressure * r
                total = u[4] + pressure
                for e in range(3):
                    bank[(PRIM + e,) + at] = vel[e]
                bank[(PRIM + 3,) + at] = heat
                axes = range(1 if flux_yz is None else 3)
                inverse = []
                for e in axes:
                    square = vel[e] * vel[e] + 1.4 * heat
                    inv = lax.rsqrt(square)
                    if e == 0:
                        bank[(SPEED,) + at] = 0.25 * (square * inv)
                    else:
                        speed_yz[(3 * e - 3,) + at] = 0.25 * (square * inv)
                    inverse.append(0.25 * inv)
                for p in range(2):
                    d = []
                    for v in range(5):
                        line = jnp.broadcast_to(table[5 * p + v : 5 * p + v + 1, :], (8, 128))
                        d.append(jnp.take_along_axis(line, shade, axis=1, mode="promise_in_bounds"))
                        bank[(SEED + 5 * p + v,) + at] = d[v]
                    dvel = [(d[1 + e] - vel[e] * d[0]) * r for e in range(3)]
                    dpress = 0.4 * (d[4] - (vel[0] * d[1] + vel[1] * d[2] + vel[2] * d[3]) + half * d[0])
                    dheat = (dpress - heat * d[0]) * r
                    for e in range(3):
                        bank[(PRIM + 4 + 4 * p + e,) + at] = dvel[e]
                    bank[(PRIM + 7 + 4 * p,) + at] = dheat
                    warm = 0.7 * dheat
                    dtotal = d[4] + dpress
                    for e in axes:
                        dspeed = (vel[e] * dvel[e] + warm) * inverse[e]
                        fluxes = []
                        for g in range(3):
                            move = d[1 + g] * vel[e] + u[1 + g] * dvel[e]
                            fluxes.append(move + dpress if g == e else move)
                        fluxes.append(dtotal * vel[e] + total * dvel[e])
                        if e == 0:
                            bank[(SPEED + 1 + p,) + at] = dspeed
                        else:
                            speed_yz[(3 * e - 2 + p,) + at] = dspeed
                        for g in range(4):
                            if e == 0:
                                bank[(FLUX + 4 * p + g,) + at] = fluxes[g]
                            else:
                                flux_yz[(8 * e - 8 + 4 * p + g,) + at] = fluxes[g]


def inviscid_yz(bank, speed_yz, flux_yz, cell, face, acc):
    places = [(l, t) for l in range(2) for t in range(2)]
    for l, t in places:
        row = BASE + 8 * t
        for p in range(2):
            for v in range(5):
                if v == 0:
                    f = get(bank, SEED + 5 * p + 2, l, row)
                else:
                    f = get(flux_yz, 4 * p + v - 1, l, row)
                put(cell, 5 * p + v, l, 8 * t, (8.0 / 12.0) * f - (1.0 / 12.0) * (ahead(f) + ahead(f, -1)))
    for l, t in places:
        row = BASE + 8 * t
        here = get(speed_yz, 0, l, row)
        s_sum = here + ahead(here)
        ds = []
        for p in range(2):
            here = get(speed_yz, 1 + p, l, row)
            ds.append(here + ahead(here))
        for v in range(5):
            here = get(bank, STATE + v, l, row)
            jump = ahead(here) - here
            for p in range(2):
                here = get(bank, SEED + 5 * p + v, l, row)
                central = get(cell, 5 * p + v, l, 8 * t)
                made = ds[p] * jump + s_sum * (ahead(here) - here) - (central + ahead(central))
                put(face, 5 * p + v, l, 8 * t, made)
    for t in range(2):
        row = BASE + 8 * t
        s_sum = get(speed_yz, 3, 0, row) + get(speed_yz, 3, 1, row)
        ds = [get(speed_yz, 4 + p, 0, row) + get(speed_yz, 4 + p, 1, row) for p in range(2)]
        for v in range(5):
            jump = get(bank, STATE + v, 1, row) - get(bank, STATE + v, 0, row)
            for p in range(2):
                if v == 0:
                    mean = get(bank, SEED + 5 * p + 3, 0, row) + get(bank, SEED + 5 * p + 3, 1, row)
                else:
                    mean = get(flux_yz, 8 + 4 * p + v - 1, 0, row) + get(flux_yz, 8 + 4 * p + v - 1, 1, row)
                djump = get(bank, SEED + 5 * p + v, 1, row) - get(bank, SEED + 5 * p + v, 0, row)
                wall = 0.5 * mean - (ds[p] * jump + s_sum * djump)
                for l in range(2):
                    made = get(face, 5 * p + v, l, 8 * t)
                    made = made - ahead(made, -1)
                    put(acc, 5 * p + v, l, 8 * t, made + wall if l == 1 else made - wall)


def stresses(bank, stress, rows):
    quarter = 0.25 * MU
    for row in rows:
        for k in range(3):
            q = PRIM + 4 * k
            grad_z = [2.0 * (get(bank, q + i, 1, row) - get(bank, q + i, 0, row)) for i in range(4 if k else 3)]
            for l in range(2):
                count = range(4 if k else 3)
                grad_x = [get(bank, q + i, l, row + 1) - get(bank, q + i, l, row - 1) for i in count]
                here = [get(bank, q + i, l, row) for i in count]
                grad_y = [ahead(h, 1) - ahead(h, -1) for h in here]
                third = (2.0 / 3.0) * (grad_x[0] + grad_y[1] + grad_z[2])
                base = 9 * k - 3 if k else 0
                put(stress, base, l, row, quarter * (2.0 * grad_x[0] - third))
                put(stress, base + 1, l, row, quarter * (grad_y[0] + grad_x[1]))
                put(stress, base + 2, l, row, quarter * (grad_z[0] + grad_x[2]))
                put(stress, base + 3, l, row, quarter * (2.0 * grad_y[1] - third))
                put(stress, base + 4, l, row, quarter * (grad_z[1] + grad_y[2]))
                put(stress, base + 5, l, row, quarter * (2.0 * grad_z[2] - third))
                if k > 0:
                    put(stress, base + 6, l, row, (0.25 * KAPPA) * grad_x[3])
                    put(stress, base + 7, l, row, (0.25 * KAPPA) * grad_y[3])
                    put(stress, base + 8, l, row, (0.25 * KAPPA) * grad_z[3])


def x_faces(bank, stress, xface, rows):
    for l in range(2):
        for row in rows:
            pair = lambda ref, f: get(ref, f, l, row) + get(ref, f, l, row + 1)
            s_sum = pair(bank, SPEED)
            ds = [pair(bank, SPEED + 1 + p) for p in range(2)]
            for v in range(5):
                jump = get(bank, STATE + v, l, row + 1) - get(bank, STATE + v, l, row)
                for p in range(2):
                    f = SEED + 5 * p + v
                    made = ds[p] * jump + s_sum * (get(bank, f, l, row + 1) - get(bank, f, l, row))
                    if v == 4:
                        work = 0.0
                        for e in range(3):
                            i = TENSOR[0][e]
                            work = work + pair(bank, PRIM + e) * pair(stress, 6 + 9 * p + i)
                            work = work + pair(bank, PRIM + 4 + 4 * p + e) * pair(stress, i)
                        made = made + 0.5 * work
                    put(xface, 5 * p + v, l, row, made)


def finish(bank, stress, xface, yface, zface, acc, flags, out):
    for t in range(2):
        row = BASE + 8 * t
        for l in range(2):
            def pair(ref, f):
                here = get(ref, f, l, row)
                return here + ahead(here)

            v_sum = [pair(bank, PRIM + e) for e in range(3)]
            t_sum = [pair(stress, i) for i in TENSOR[1]]
            for p in range(2):
                work = 0.0
                for e in range(3):
                    work = work + v_sum[e] * pair(stress, 6 + 9 * p + TENSOR[1][e])
                    work = work + pair(bank, PRIM + 4 + 4 * p + e) * t_sum[e]
                put(yface, p, l, 8 * t, 0.5 * work)
        both = lambda ref, f: get(ref, f, 0, row) + get(ref, f, 1, row)
        v_sum = [both(bank, PRIM + e) for e in range(3)]
        t_sum = [both(stress, i) for i in TENSOR[2]]
        for p in range(2):
            work = 0.0
            for e in range(3):
                dt = both(stress, 6 + 9 * p + TENSOR[2][e])
                put(zface, 4 * p + e, 0, 8 * t, dt)
                work = work + v_sum[e] * dt + both(bank, PRIM + 4 + 4 * p + e) * t_sum[e]
            put(zface, 4 * p + 3, 0, 8 * t, 0.5 * work + both(stress, 6 + 9 * p + 8))
    for t in range(2):
        row = BASE + 8 * t
        solid = flags(8 * t) == 1
        for l in range(2):
            for p in range(2):
                for v in range(5):
                    f = SEED + 5 * p + 1 if v == 0 else FLUX + 4 * p + v - 1
                    total = get(acc, 5 * p + v, l, 8 * t)
                    total = total - (8.0 / 12.0) * (get(bank, f, l, row + 1) - get(bank, f, l, row - 1))
                    total = total + (1.0 / 12.0) * (get(bank, f, l, row + 2) - get(bank, f, l, row - 2))
                    total = total + get(xface, 5 * p + v, l, row) - get(xface, 5 * p + v, l, row - 1)
                    if v > 0:
                        f = 6 + 9 * p + (6 if v == 4 else TENSOR[0][v - 1])
                        total = total + get(stress, f, l, row + 1) - get(stress, f, l, row - 1)
                        here = get(stress, 6 + 9 * p + (7 if v == 4 else TENSOR[1][v - 1]), l, row)
                        if v == 4:
                            work = get(yface, p, l, 8 * t)
                            total = total + ahead(here) + work - ahead(here + work, -1)
                        else:
                            total = total + ahead(here) - ahead(here, -1)
                        wall = get(zface, 4 * p + v - 1, 0, 8 * t)
                        total = total + wall if l == 0 else total - wall
                    put(out, 5 * p + v, l, 8 * t, jnp.where(solid, -get(bank, SEED + 5 * p + v, l, row), total))


def pack_x(flow, colour, flags, weights, to_near, to_far, flow_out, colour_out, flags_out, weights_out, sems):
    pairs = ((flow, flow_out), (colour, colour_out), (flags, flags_out), (weights, weights_out))
    copies = [pltpu.make_async_copy(src, dst, sems.at[i]) for i, (src, dst) in enumerate(pairs)]
    for copy in copies:
        copy.start()
    for copy in copies:
        copy.wait()
    odd = lax.rem(lax.axis_index("gx"), 2)

    def fill(dst, start):
        for l in range(2):
            for v in range(5):
                dst[4 * v + 2 * l : 4 * v + 2 * l + 2, :] = flow_out[v, l, start : start + 2, :]
            dst[20 + 2 * l : 22 + 2 * l, :] = colour_out[l, start : start + 2, :].astype(jnp.float32)

    @pl.when(odd == 0)
    def _():
        fill(to_near, 14)
        fill(to_far, 0)

    @pl.when(odd == 1)
    def _():
        fill(to_near, 0)
        fill(to_far, 14)


def own_cells(flow, colour, weights, bank, acc, table, speed_yz, flux_yz, cell, face):
    for p in range(2):
        for v in range(5):
            line = weights[v, p : p + 1, :]
            table[5 * p + v : 5 * p + v + 1, :] = jnp.concatenate([line, jnp.zeros((1, 101), jnp.float32)], axis=1)
    for l in range(2):
        for c in range(4):
            lanes = slice(128 * c, 128 * c + 128)
            for v in range(5):
                bank[STATE + v, l, c, BASE : BASE + 16, :] = flow[v, l, :, lanes]
            bank[STATE + 5, l, c, BASE : BASE + 16, :] = colour[l, :, lanes].astype(jnp.float32)
    pointwise(bank, table, (BASE, BASE + 8), speed_yz, flux_yz)
    inviscid_yz(bank, speed_yz, flux_yz, cell, face, acc)


def x_halo(near, far, store):
    odd = lax.rem(lax.axis_index("gx"), 2)

    def fill(src, row):
        for l in range(2):
            for v in range(6):
                store(v, l, row, src, 4 * v + 2 * l)

    @pl.when(odd == 0)
    def _():
        fill(far, BASE - 2)
        fill(near, BASE + 16)

    @pl.when(odd == 1)
    def _():
        fill(near, BASE - 2)
        fill(far, BASE + 16)


def pack_y(flow, colour, near, far, table, edge, to_near, to_far):
    for l in range(2):
        for side in range(2):
            lanes = slice(384 * side, 384 * side + 128)
            for v in range(5):
                edge[v, l, side, BASE : BASE + 16, :] = flow[v, l, :, lanes]
            edge[5, l, side, BASE : BASE + 16, :] = colour[l, :, lanes].astype(jnp.float32)

    def store(v, l, row, src, at):
        for side in range(2):
            edge[v, l, side, row : row + 2, :] = src[at : at + 2, 384 * side : 384 * side + 128]

    x_halo(near, far, store)
    lane = lax.broadcasted_iota(jnp.int32, (24, 128), 1)

    def columns(side, first):
        made = jnp.zeros((24, 128), jnp.float32)
        for l in range(2):
            for v in range(6):
                at = 2 * (6 * l + v)
                moved = pltpu.roll(edge[v, l, side, BASE - 4 : BASE + 20, :], (at - first) % 128, 1)
                made = jnp.where((lane >= at) & (lane < at + 2), moved, made)
        return made

    left, right = columns(0, 0), columns(1, 126)
    odd = lax.rem(lax.axis_index("gy"), 2)

    @pl.when(odd == 0)
    def _():
        to_near[...] = right
        to_far[...] = left

    @pl.when(odd == 1)
    def _():
        to_near[...] = left
        to_far[...] = right


def whole_rows(near, far, table, flags, bank_in, acc, bank, result, out, stress, xface, yface, zface, sem):
    def store(v, l, row, src, at):
        for c in range(4):
            bank[STATE + v, l, c, row : row + 2, :] = src[at : at + 2, 128 * c : 128 * c + 128]

    x_halo(near, far, store)
    pointwise(bank, table, (BASE - 4, BASE + 12))
    rows = (BASE - 4, BASE + 4, BASE + 12)
    stresses(bank, stress, rows)
    x_faces(bank, stress, xface, rows)
    finish(bank, stress, xface, yface, zface, acc, lambda row: flags[row : row + 8, :], result)
    copies = []
    for c in (1, 2):
        copies.append(
            pltpu.make_async_copy(result.at[:, :, c], out.at[:, :, :, 128 * c : 128 * c + 128], sem.at[c - 1])
        )
        copies[-1].start()
    for copy in copies:
        copy.wait()


def edge_columns(
    near, far, edge, table, flags, result, out_in, out, bank, acc, speed_yz, flux_yz, cell, face, stress, xface, yface,
    zface, final, staged, sem,
):
    lane = lax.broadcasted_iota(jnp.int32, (24, 128), 1)
    odd = lax.rem(lax.axis_index("gy"), 2)

    def unpack(low, high):
        for l in range(2):
            for v in range(6):
                at = 2 * (6 * l + v)
                first = edge[v, l, 0, BASE - 4 : BASE + 20, :]
                last = pltpu.roll(edge[v, l, 1, BASE - 4 : BASE + 20, :], 64, 1)
                below = pltpu.roll(low[...], (126 - at) % 128, 1)
                above = pltpu.roll(high[...], 64 - at, 1)
                made = jnp.where(lane < 32, first, last)
                made = jnp.where(lane >= 64, above, made)
                bank[STATE + v, l, 0, BASE - 4 : BASE + 20, :] = jnp.where(lane >= 96, below, made)

    @pl.when(odd == 0)
    def _():
        unpack(far, near)

    @pl.when(odd == 1)
    def _():
        unpack(near, far)

    rows = (BASE - 4, BASE + 4, BASE + 12)
    pointwise(bank, table, rows, speed_yz, flux_yz)
    inviscid_yz(bank, speed_yz, flux_yz, cell, face, acc)
    stresses(bank, stress, rows)
    x_faces(bank, stress, xface, rows)
    column = lax.broadcasted_iota(jnp.int32, (8, 128), 1)

    def solid(row):
        last = pltpu.roll(flags[row : row + 8, 384:512], 64, 1)
        return jnp.where(column < 32, flags[row : row + 8, 0:128], last)

    finish(bank, stress, xface, yface, zface, acc, solid, final)
    for f in range(10):
        for l in range(2):
            for t in range(2):
                rows = slice(8 * t, 8 * t + 8)
                made = final[f, l, 0, rows, :]
                staged[0, f, l, rows, :] = jnp.where(column < 2, made, result[f, l, 0, rows, :])
                made = pltpu.roll(made, 64, 1)
                staged[1, f, l, rows, :] = jnp.where(column >= 126, made, result[f, l, 3, rows, :])
    copies = []
    for side in range(2):
        lanes = slice(384 * side, 384 * side + 128)
        copies.append(pltpu.make_async_copy(staged.at[side], out.at[:, :, :, lanes], sem.at[side]))
        copies[-1].start()
    for copy in copies:
        copy.wait()


def swap(value, axis, offset):
    count = lax.axis_size(axis)
    pairs = []
    for k in range(0, count, 2):
        i, j = (k + offset) % count, (k + offset + 1) % count
        pairs += [(i, j), (j, i)]
    return lax.ppermute(value, axis, pairs)


def local(flow_state, colour_map, cell_flags, probe_weights):
    f32 = jnp.float32
    vmem = pl.BlockSpec(memory_space=pltpu.VMEM)
    hbm = pl.BlockSpec(memory_space=pltpu.HBM)

    def call(kernel, ins, outs, scratch=(), alias={}, cost=0):
        return pl.pallas_call(
            kernel,
            out_shape=[jax.ShapeDtypeStruct(s, d) for s, d, _ in outs],
            in_specs=ins,
            out_specs=[m for _, _, m in outs],
            scratch_shapes=scratch,
            input_output_aliases=alias,
            compiler_params=pltpu.CompilerParams(vmem_limit_bytes=24 * 1024 * 1024),
            cost_estimate=pl.CostEstimate(flops=cost, bytes_accessed=cost, transcendentals=0),
        )

    def banks(n, tiles, rows=ROWS):
        return pltpu.VMEM((n, 2, tiles, rows, 128), f32)

    inputs = [flow_state, colour_map, cell_flags, jnp.transpose(probe_weights, (2, 0, 1))]
    x_near, x_far, flow, colour, flags, weights = call(
        pack_x,
        [hbm] * 4,
        [((24, 512), f32, vmem)] * 2 + [(x.shape, x.dtype, vmem) for x in inputs],
        [pltpu.SemaphoreType.DMA((4,))],
    )(*[pltpu.with_memory_space_constraint(x, pltpu.HBM) for x in inputs])
    x_far = swap(x_far, "gx", 1)
    x_near = swap(x_near, "gx", 0)
    bank, acc, table = call(
        own_cells,
        [vmem] * 3,
        [((FIELDS, 2, 4, ROWS, 128), f32, vmem), ((10, 2, 4, 16, 128), f32, vmem), ((16, 128), f32, vmem)],
        [banks(6, 4), banks(16, 4), banks(10, 4, 16), banks(10, 4, 16)],
        cost=8000000,
    )(flow, colour, weights)
    edge, y_near, y_far = call(
        pack_y,
        [vmem] * 5,
        [((6, 2, 2, ROWS, 128), f32, vmem), ((24, 128), f32, vmem), ((24, 128), f32, vmem)],
    )(flow, colour, x_near, x_far, table)
    y_far = swap(y_far, "gy", 1)
    y_near = swap(y_near, "gy", 0)
    bank, result, out = call(
        whole_rows,
        [vmem] * 6,
        [(bank.shape, f32, vmem), (acc.shape, f32, vmem), ((10, 2, 16, 512), f32, hbm)],
        [banks(24, 4), banks(10, 4), banks(2, 4, 16), pltpu.VMEM((8, 1, 4, 16, 128), f32), pltpu.SemaphoreType.DMA((2,))],
        alias={4: 0, 5: 1},
        cost=8000000,
    )(x_near, x_far, table, flags, bank, acc)
    (out,) = call(
        edge_columns,
        [vmem] * 6 + [hbm],
        [(out.shape, f32, hbm)],
        [
            banks(FIELDS, 1),
            banks(10, 1, 16),
            banks(6, 1),
            banks(16, 1),
            banks(10, 1, 16),
            banks(10, 1, 16),
            banks(24, 1),
            banks(10, 1),
            banks(2, 1, 16),
            pltpu.VMEM((8, 1, 1, 16, 128), f32),
            banks(10, 1, 16),
            pltpu.VMEM((2, 10, 2, 16, 128), f32),
            pltpu.SemaphoreType.DMA((2,)),
        ],
        alias={6: 0},
    )(y_near, y_far, edge, table, flags, result, out)
    return out.reshape(2, 5, 2, 16, 512)


def solution(mesh):
    return jax.shard_map(
        local,
        mesh=mesh,
        in_specs=(P(None, None, "gx", "gy"), P(None, "gx", "gy"), P("gx", "gy"), P()),
        out_specs=P(None, None, None, "gx", "gy"),
        check_vma=False,
    )
```

```python
import jax
import jax.numpy as jnp
from jax import lax
from jax.experimental import pallas as pl
from jax.experimental.pallas import tpu as pltpu
from jax.sharding import PartitionSpec as P

MU = 0.2
KAPPA = 0.2 * 1.4 / (0.4 * 0.72)
BASE = 12
ROWS = 40
STATE, SEED, PRIM, SPEED, FLUX, FIELDS = 0, 6, 16, 28, 31, 39
TENSOR = ((0, 1, 2), (1, 3, 4), (2, 4, 5))


def get(ref, f, l, row):
    tiles = [ref[f, l, c, row : row + 8, :] for c in range(ref.shape[2])]
    return tiles[0] if len(tiles) == 1 else jnp.concatenate(tiles, axis=1)


def put(ref, f, l, row, value):
    for c in range(ref.shape[2]):
        ref[f, l, c, row : row + 8, :] = value[:, 128 * c : 128 * c + 128]


def ahead(value, step=1):
    return pltpu.roll(value, (-step) % value.shape[1], 1)


def pointwise(bank, table, rows, speed_yz=None, flux_yz=None):
    for l in range(2):
        for row in rows:
            for c in range(bank.shape[2]):
                at = (l, c, slice(row, row + 8), slice(None))
                u = [bank[(STATE + v,) + at] for v in range(5)]
                shade = bank[(STATE + 5,) + at].astype(jnp.int32) & 127
                r = 1.0 / u[0]
                vel = [u[1 + e] * r for e in range(3)]
                half = 0.5 * (vel[0] * vel[0] + vel[1] * vel[1] + vel[2] * vel[2])
                pressure = 0.4 * (u[4] - half * u[0])
                heat = pressure * r
                total = u[4] + pressure
                for e in range(3):
                    bank[(PRIM + e,) + at] = vel[e]
                bank[(PRIM + 3,) + at] = heat
                axes = range(1 if flux_yz is None else 3)
                inverse = []
                for e in axes:
                    square = vel[e] * vel[e] + 1.4 * heat
                    inv = lax.rsqrt(square)
                    if e == 0:
                        bank[(SPEED,) + at] = 0.25 * (square * inv)
                    else:
                        speed_yz[(3 * e - 3,) + at] = 0.25 * (square * inv)
                    inverse.append(0.25 * inv)
                for p in range(2):
                    d = []
                    for v in range(5):
                        line = jnp.broadcast_to(table[5 * p + v : 5 * p + v + 1, :], (8, 128))
                        d.append(jnp.take_along_axis(line, shade, axis=1, mode="promise_in_bounds"))
                        bank[(SEED + 5 * p + v,) + at] = d[v]
                    dvel = [(d[1 + e] - vel[e] * d[0]) * r for e in range(3)]
                    dpress = 0.4 * (d[4] - (vel[0] * d[1] + vel[1] * d[2] + vel[2] * d[3]) + half * d[0])
                    dheat = (dpress - heat * d[0]) * r
                    for e in range(3):
                        bank[(PRIM + 4 + 4 * p + e,) + at] = dvel[e]
                    bank[(PRIM + 7 + 4 * p,) + at] = dheat
                    warm = 0.7 * dheat
                    dtotal = d[4] + dpress
                    for e in axes:
                        dspeed = (vel[e] * dvel[e] + warm) * inverse[e]
                        fluxes = []
                        for g in range(3):
                            move = d[1 + g] * vel[e] + u[1 + g] * dvel[e]
                            fluxes.append(move + dpress if g == e else move)
                        fluxes.append(dtotal * vel[e] + total * dvel[e])
                        if e == 0:
                            bank[(SPEED + 1 + p,) + at] = dspeed
                        else:
                            speed_yz[(3 * e - 2 + p,) + at] = dspeed
                        for g in range(4):
                            if e == 0:
                                bank[(FLUX + 4 * p + g,) + at] = fluxes[g]
                            else:
                                flux_yz[(8 * e - 8 + 4 * p + g,) + at] = fluxes[g]


def inviscid_yz(bank, speed_yz, flux_yz, cell, face, acc):
    places = [(l, t) for l in range(2) for t in range(2)]
    for l, t in places:
        row = BASE + 8 * t
        for p in range(2):
            for v in range(5):
                if v == 0:
                    f = get(bank, SEED + 5 * p + 2, l, row)
                else:
                    f = get(flux_yz, 4 * p + v - 1, l, row)
                put(cell, 5 * p + v, l, 8 * t, (8.0 / 12.0) * f - (1.0 / 12.0) * (ahead(f) + ahead(f, -1)))
    for l, t in places:
        row = BASE + 8 * t
        here = get(speed_yz, 0, l, row)
        s_sum = here + ahead(here)
        ds = []
        for p in range(2):
            here = get(speed_yz, 1 + p, l, row)
            ds.append(here + ahead(here))
        for v in range(5):
            here = get(bank, STATE + v, l, row)
            jump = ahead(here) - here
            for p in range(2):
                here = get(bank, SEED + 5 * p + v, l, row)
                central = get(cell, 5 * p + v, l, 8 * t)
                made = ds[p] * jump + s_sum * (ahead(here) - here) - (central + ahead(central))
                put(face, 5 * p + v, l, 8 * t, made)
    for t in range(2):
        row = BASE + 8 * t
        s_sum = get(speed_yz, 3, 0, row) + get(speed_yz, 3, 1, row)
        ds = [get(speed_yz, 4 + p, 0, row) + get(speed_yz, 4 + p, 1, row) for p in range(2)]
        for v in range(5):
            jump = get(bank, STATE + v, 1, row) - get(bank, STATE + v, 0, row)
            for p in range(2):
                if v == 0:
                    mean = get(bank, SEED + 5 * p + 3, 0, row) + get(bank, SEED + 5 * p + 3, 1, row)
                else:
                    mean = get(flux_yz, 8 + 4 * p + v - 1, 0, row) + get(flux_yz, 8 + 4 * p + v - 1, 1, row)
                djump = get(bank, SEED + 5 * p + v, 1, row) - get(bank, SEED + 5 * p + v, 0, row)
                wall = 0.5 * mean - (ds[p] * jump + s_sum * djump)
                for l in range(2):
                    made = get(face, 5 * p + v, l, 8 * t)
                    made = made - ahead(made, -1)
                    put(acc, 5 * p + v, l, 8 * t, made + wall if l == 1 else made - wall)


def stresses(bank, stress, rows):
    quarter = 0.25 * MU
    for row in rows:
        for k in range(3):
            q = PRIM + 4 * k
            grad_z = [2.0 * (get(bank, q + i, 1, row) - get(bank, q + i, 0, row)) for i in range(4 if k else 3)]
            for l in range(2):
                count = range(4 if k else 3)
                grad_x = [get(bank, q + i, l, row + 1) - get(bank, q + i, l, row - 1) for i in count]
                here = [get(bank, q + i, l, row) for i in count]
                grad_y = [ahead(h, 1) - ahead(h, -1) for h in here]
                third = (2.0 / 3.0) * (grad_x[0] + grad_y[1] + grad_z[2])
                base = 9 * k - 3 if k else 0
                put(stress, base, l, row, quarter * (2.0 * grad_x[0] - third))
                put(stress, base + 1, l, row, quarter * (grad_y[0] + grad_x[1]))
                put(stress, base + 2, l, row, quarter * (grad_z[0] + grad_x[2]))
                put(stress, base + 3, l, row, quarter * (2.0 * grad_y[1] - third))
                put(stress, base + 4, l, row, quarter * (grad_z[1] + grad_y[2]))
                put(stress, base + 5, l, row, quarter * (2.0 * grad_z[2] - third))
                if k > 0:
                    put(stress, base + 6, l, row, (0.25 * KAPPA) * grad_x[3])
                    put(stress, base + 7, l, row, (0.25 * KAPPA) * grad_y[3])
                    put(stress, base + 8, l, row, (0.25 * KAPPA) * grad_z[3])


def x_faces(bank, stress, xface, rows):
    for l in range(2):
        for row in rows:
            pair = lambda ref, f: get(ref, f, l, row) + get(ref, f, l, row + 1)
            s_sum = pair(bank, SPEED)
            ds = [pair(bank, SPEED + 1 + p) for p in range(2)]
            for v in range(5):
                jump = get(bank, STATE + v, l, row + 1) - get(bank, STATE + v, l, row)
                for p in range(2):
                    f = SEED + 5 * p + v
                    made = ds[p] * jump + s_sum * (get(bank, f, l, row + 1) - get(bank, f, l, row))
                    if v == 4:
                        work = 0.0
                        for e in range(3):
                            i = TENSOR[0][e]
                            work = work + pair(bank, PRIM + e) * pair(stress, 6 + 9 * p + i)
                            work = work + pair(bank, PRIM + 4 + 4 * p + e) * pair(stress, i)
                        made = made + 0.5 * work
                    put(xface, 5 * p + v, l, row, made)


def finish(bank, stress, xface, yface, ypart, zface, acc, flags, emit):
    for t in range(2):
        row = BASE + 8 * t
        for l in range(2):
            def pair(ref, f):
                here = get(ref, f, l, row)
                return here + ahead(here)

            v_sum = [pair(bank, PRIM + e) for e in range(3)]
            t_sum = [pair(stress, i) for i in TENSOR[1]]
            for p in range(2):
                work = 0.0
                for e in range(3):
                    here = get(stress, 6 + 9 * p + TENSOR[1][e], l, row)
                    after = ahead(here)
                    put(ypart, 4 * p + e, l, 8 * t, after - ahead(here, -1))
                    work = work + v_sum[e] * (here + after)
                    work = work + pair(bank, PRIM + 4 + 4 * p + e) * t_sum[e]
                put(yface, p, l, 8 * t, 0.5 * work)
        both = lambda ref, f: get(ref, f, 0, row) + get(ref, f, 1, row)
        v_sum = [both(bank, PRIM + e) for e in range(3)]
        t_sum = [both(stress, i) for i in TENSOR[2]]
        for p in range(2):
            work = 0.0
            for e in range(3):
                dt = both(stress, 6 + 9 * p + TENSOR[2][e])
                put(zface, 4 * p + e, 0, 8 * t, dt)
                work = work + v_sum[e] * dt + both(bank, PRIM + 4 + 4 * p + e) * t_sum[e]
            put(zface, 4 * p + 3, 0, 8 * t, 0.5 * work + both(stress, 6 + 9 * p + 8))
    for t in range(2):
        for l in range(2):
            for p in range(2):
                here = get(stress, 13 + 9 * p, l, BASE + 8 * t)
                work = get(yface, p, l, 8 * t)
                put(ypart, 4 * p + 3, l, 8 * t, ahead(here) + work - ahead(here + work, -1))
    solid = [flags(8 * t) == 1 for t in range(2)]
    for p in range(2):
        for v in range(5):
            for l in range(2):
                for t in range(2):
                    row = BASE + 8 * t
                    f = SEED + 5 * p + 1 if v == 0 else FLUX + 4 * p + v - 1
                    near = get(bank, f, l, row + 1) - get(bank, f, l, row - 1)
                    far = get(bank, f, l, row + 2) - get(bank, f, l, row - 2)
                    face = get(xface, 5 * p + v, l, row) - get(xface, 5 * p + v, l, row - 1)
                    total = get(acc, 5 * p + v, l, 8 * t) + face - (8.0 / 12.0) * near + (1.0 / 12.0) * far
                    if v > 0:
                        f = 6 + 9 * p + (6 if v == 4 else TENSOR[0][v - 1])
                        viscous = get(stress, f, l, row + 1) - get(stress, f, l, row - 1)
                        viscous = viscous + get(ypart, 4 * p + v - 1, l, 8 * t)
                        wall = get(zface, 4 * p + v - 1, 0, 8 * t)
                        total = total + (viscous + wall if l == 0 else viscous - wall)
                    value = jnp.where(solid[t], -get(bank, SEED + 5 * p + v, l, row), total)
                    emit(5 * p + v, l, 8 * t, value)


def pack_x(flow, colour, flags, weights, to_far, to_near, flow_out, colour_out, flags_out, weights_out, sems):
    pairs = ((flow, flow_out), (colour, colour_out), (flags, flags_out), (weights, weights_out))
    copies = [pltpu.make_async_copy(src, dst, sems.at[i]) for i, (src, dst) in enumerate(pairs)]
    for copy in copies:
        copy.start()
    for copy in copies:
        copy.wait()
    odd = lax.rem(lax.axis_index("gx"), 2)

    def fill(dst, start):
        for l in range(2):
            for v in range(5):
                dst[4 * v + 2 * l : 4 * v + 2 * l + 2, :] = flow_out[v, l, start : start + 2, :]
            dst[20 + 2 * l : 22 + 2 * l, :] = colour_out[l, start : start + 2, :].astype(jnp.float32)

    @pl.when(odd == 0)
    def _():
        fill(to_near, 14)
        fill(to_far, 0)

    @pl.when(odd == 1)
    def _():
        fill(to_near, 0)
        fill(to_far, 14)


def own_cells(flow, colour, weights, bank, acc, table, speed_yz, flux_yz, cell, face):
    for p in range(2):
        for v in range(5):
            line = weights[v, p : p + 1, :]
            table[5 * p + v : 5 * p + v + 1, :] = jnp.concatenate([line, jnp.zeros((1, 101), jnp.float32)], axis=1)
    for l in range(2):
        for c in range(4):
            lanes = slice(128 * c, 128 * c + 128)
            for v in range(5):
                bank[STATE + v, l, c, BASE : BASE + 16, :] = flow[v, l, :, lanes]
            bank[STATE + 5, l, c, BASE : BASE + 16, :] = colour[l, :, lanes].astype(jnp.float32)
    pointwise(bank, table, (BASE, BASE + 8), speed_yz, flux_yz)
    inviscid_yz(bank, speed_yz, flux_yz, cell, face, acc)


def x_halo(near, far, store):
    odd = lax.rem(lax.axis_index("gx"), 2)

    def fill(src, row):
        for l in range(2):
            for v in range(6):
                store(v, l, row, src, 4 * v + 2 * l)

    @pl.when(odd == 0)
    def _():
        fill(far, BASE - 2)
        fill(near, BASE + 16)

    @pl.when(odd == 1)
    def _():
        fill(near, BASE - 2)
        fill(far, BASE + 16)


def pack_y(flow, colour, far, near, table, edge, to_far, to_near):
    for l in range(2):
        for side in range(2):
            lanes = slice(384 * side, 384 * side + 128)
            for v in range(5):
                edge[v, l, side, BASE : BASE + 16, :] = flow[v, l, :, lanes]
            edge[5, l, side, BASE : BASE + 16, :] = colour[l, :, lanes].astype(jnp.float32)

    def store(v, l, row, src, at):
        for side in range(2):
            edge[v, l, side, row : row + 2, :] = src[at : at + 2, 384 * side : 384 * side + 128]

    x_halo(near, far, store)
    lane = lax.broadcasted_iota(jnp.int32, (24, 128), 1)

    def columns(side, first):
        made = jnp.zeros((24, 128), jnp.float32)
        for l in range(2):
            for v in range(6):
                at = 2 * (6 * l + v)
                moved = pltpu.roll(edge[v, l, side, BASE - 4 : BASE + 20, :], (at - first) % 128, 1)
                made = jnp.where((lane >= at) & (lane < at + 2), moved, made)
        return made

    left, right = columns(0, 0), columns(1, 126)
    odd = lax.rem(lax.axis_index("gy"), 2)

    @pl.when(odd == 0)
    def _():
        to_near[...] = right
        to_far[...] = left

    @pl.when(odd == 1)
    def _():
        to_near[...] = left
        to_far[...] = right


def whole_rows(far, near, table, flags, bank_in, acc, bank, result, stress, xface, yface, ypart, zface):
    def store(v, l, row, src, at):
        for c in range(4):
            bank[STATE + v, l, c, row : row + 2, :] = src[at : at + 2, 128 * c : 128 * c + 128]

    x_halo(near, far, store)
    pointwise(bank, table, (BASE - 4, BASE + 12))
    rows = (BASE - 4, BASE + 4, BASE + 12)
    stresses(bank, stress, rows)
    x_faces(bank, stress, xface, rows)
    solid = lambda row: flags[row : row + 8, :]
    emit = lambda f, l, row, value: put(result, f, l, row, value)
    finish(bank, stress, xface, yface, ypart, zface, acc, solid, emit)


def edge_columns(
    far, near, edge, table, flags, result, out, bank, acc, speed_yz, flux_yz, cell, face, stress, xface, yface, ypart,
    zface, staged, middle_sem, edge_sem,
):
    middle = []
    for c in (1, 2):
        lanes = slice(128 * c, 128 * c + 128)
        middle.append(pltpu.make_async_copy(result.at[:, :, c], out.at[:, :, :, lanes], middle_sem.at[c - 1]))
        middle[-1].start()
    lane = lax.broadcasted_iota(jnp.int32, (24, 128), 1)
    odd = lax.rem(lax.axis_index("gy"), 2)

    def unpack(low, high):
        for l in range(2):
            for v in range(6):
                at = 2 * (6 * l + v)
                first = edge[v, l, 0, BASE - 4 : BASE + 20, :]
                last = pltpu.roll(edge[v, l, 1, BASE - 4 : BASE + 20, :], 64, 1)
                below = pltpu.roll(low[...], (126 - at) % 128, 1)
                above = pltpu.roll(high[...], 64 - at, 1)
                made = jnp.where(lane < 32, first, last)
                made = jnp.where(lane >= 64, above, made)
                bank[STATE + v, l, 0, BASE - 4 : BASE + 20, :] = jnp.where(lane >= 96, below, made)

    @pl.when(odd == 0)
    def _():
        unpack(far, near)

    @pl.when(odd == 1)
    def _():
        unpack(near, far)

    rows = (BASE - 4, BASE + 4, BASE + 12)
    pointwise(bank, table, rows, speed_yz, flux_yz)
    inviscid_yz(bank, speed_yz, flux_yz, cell, face, acc)
    stresses(bank, stress, rows)
    x_faces(bank, stress, xface, rows)
    column = lax.broadcasted_iota(jnp.int32, (8, 128), 1)

    def solid(row):
        last = pltpu.roll(flags[row : row + 8, 384:512], 64, 1)
        return jnp.where(column < 32, flags[row : row + 8, 0:128], last)

    copies = []

    def emit(f, l, row, made):
        rows = slice(row, row + 8)
        staged[0, f, l, rows, :] = jnp.where(column < 2, made, result[f, l, 0, rows, :])
        staged[1, f, l, rows, :] = jnp.where(column >= 126, pltpu.roll(made, 64, 1), result[f, l, 3, rows, :])
        if l == 1 and row == 8:
            for side in range(2):
                lanes = slice(384 * side, 384 * side + 128)
                copies.append(pltpu.make_async_copy(staged.at[side, f], out.at[f, :, :, lanes], edge_sem.at[side, f]))
                copies[-1].start()

    finish(bank, stress, xface, yface, ypart, zface, acc, solid, emit)
    for copy in middle + copies:
        copy.wait()


def swap(value, axis, offset):
    count = lax.axis_size(axis)
    pairs = []
    for k in range(0, count, 2):
        i, j = (k + offset) % count, (k + offset + 1) % count
        pairs += [(i, j), (j, i)]
    return lax.ppermute(value, axis, pairs)


def local(flow_state, colour_map, cell_flags, probe_weights):
    f32 = jnp.float32
    vmem = pl.BlockSpec(memory_space=pltpu.VMEM)
    hbm = pl.BlockSpec(memory_space=pltpu.HBM)

    def call(kernel, ins, outs, scratch=(), alias={}, cost=0):
        return pl.pallas_call(
            kernel,
            out_shape=[jax.ShapeDtypeStruct(s, d) for s, d, _ in outs],
            in_specs=ins,
            out_specs=[m for _, _, m in outs],
            scratch_shapes=scratch,
            input_output_aliases=alias,
            compiler_params=pltpu.CompilerParams(vmem_limit_bytes=24 * 1024 * 1024),
            cost_estimate=pl.CostEstimate(flops=cost, bytes_accessed=cost, transcendentals=0),
        )

    def banks(n, tiles, rows=ROWS):
        return pltpu.VMEM((n, 2, tiles, rows, 128), f32)

    inputs = [flow_state, colour_map, cell_flags, jnp.transpose(probe_weights, (2, 0, 1))]
    x_far, x_near, flow, colour, flags, weights = call(
        pack_x,
        [hbm] * 4,
        [((24, 512), f32, vmem)] * 2 + [(x.shape, x.dtype, vmem) for x in inputs],
        [pltpu.SemaphoreType.DMA((4,))],
    )(*[pltpu.with_memory_space_constraint(x, pltpu.HBM) for x in inputs])
    x_far = swap(x_far, "gx", 1)
    x_near = swap(x_near, "gx", 0)
    bank, acc, table = call(
        own_cells,
        [vmem] * 3,
        [((FIELDS, 2, 4, ROWS, 128), f32, vmem), ((10, 2, 4, 16, 128), f32, vmem), ((16, 128), f32, vmem)],
        [banks(6, 4), banks(16, 4), banks(10, 4, 16), banks(10, 4, 16)],
        cost=8000000,
    )(flow, colour, weights)
    edge, y_far, y_near = call(
        pack_y,
        [vmem] * 5,
        [((6, 2, 2, ROWS, 128), f32, vmem), ((24, 128), f32, vmem), ((24, 128), f32, vmem)],
    )(flow, colour, x_far, x_near, table)
    y_far = swap(y_far, "gy", 1)
    y_near = swap(y_near, "gy", 0)
    bank, result = call(
        whole_rows,
        [vmem] * 6,
        [(bank.shape, f32, vmem), (acc.shape, f32, vmem)],
        [banks(24, 4), banks(10, 4), banks(2, 4, 16), banks(8, 4, 16), pltpu.VMEM((8, 1, 4, 16, 128), f32)],
        alias={4: 0, 5: 1},
        cost=8000000,
    )(x_far, x_near, table, flags, bank, acc)
    (out,) = call(
        edge_columns,
        [vmem] * 6,
        [((10, 2, 16, 512), f32, hbm)],
        [
            banks(FIELDS, 1),
            banks(10, 1, 16),
            banks(6, 1),
            banks(16, 1),
            banks(10, 1, 16),
            banks(10, 1, 16),
            banks(24, 1),
            banks(10, 1),
            banks(2, 1, 16),
            banks(8, 1, 16),
            pltpu.VMEM((8, 1, 1, 16, 128), f32),
            pltpu.VMEM((2, 10, 2, 16, 128), f32),
            pltpu.SemaphoreType.DMA((2,)),
            pltpu.SemaphoreType.DMA((2, 10)),
        ],
    )(y_far, y_near, edge, table, flags, result)
    return out.reshape(2, 5, 2, 16, 512)


def solution(mesh):
    return jax.shard_map(
        local,
        mesh=mesh,
        in_specs=(P(None, None, "gx", "gy"), P(None, "gx", "gy"), P("gx", "gy"), P()),
        out_specs=P(None, None, None, "gx", "gy"),
        check_vma=False,
    )
```

```python
import jax
import jax.numpy as jnp
from jax import lax
from jax.experimental import pallas as pl
from jax.experimental.pallas import tpu as pltpu
from jax.sharding import PartitionSpec as P

MU = 0.2
KAPPA = 0.2 * 1.4 / (0.4 * 0.72)
BASE = 12
ROWS = 40
STATE, SEED, PRIM, SPEED, FLUX, FIELDS = 0, 6, 16, 28, 31, 39
TENSOR = ((0, 1, 2), (1, 3, 4), (2, 4, 5))


def get(ref, f, l, row):
    tiles = [ref[f, l, c, row : row + 8, :] for c in range(ref.shape[2])]
    return tiles[0] if len(tiles) == 1 else jnp.concatenate(tiles, axis=1)


def put(ref, f, l, row, value):
    for c in range(ref.shape[2]):
        ref[f, l, c, row : row + 8, :] = value[:, 128 * c : 128 * c + 128]


def ahead(value, step=1):
    return pltpu.roll(value, (-step) % value.shape[1], 1)


def pointwise(bank, table, rows, speed_yz=None, flux_yz=None):
    for l in range(2):
        for row in rows:
            for c in range(bank.shape[2]):
                at = (l, c, slice(row, row + 8), slice(None))
                u = [bank[(STATE + v,) + at] for v in range(5)]
                shade = bank[(STATE + 5,) + at].astype(jnp.int32) & 127
                r = 1.0 / u[0]
                vel = [u[1 + e] * r for e in range(3)]
                half = 0.5 * (vel[0] * vel[0] + vel[1] * vel[1] + vel[2] * vel[2])
                pressure = 0.4 * (u[4] - half * u[0])
                heat = pressure * r
                total = u[4] + pressure
                for e in range(3):
                    bank[(PRIM + e,) + at] = vel[e]
                bank[(PRIM + 3,) + at] = heat
                axes = range(1 if flux_yz is None else 3)
                inverse = []
                for e in axes:
                    square = vel[e] * vel[e] + 1.4 * heat
                    inv = lax.rsqrt(square)
                    if e == 0:
                        bank[(SPEED,) + at] = 0.25 * (square * inv)
                    else:
                        speed_yz[(3 * e - 3,) + at] = 0.25 * (square * inv)
                    inverse.append(0.25 * inv)
                for p in range(2):
                    d = []
                    for v in range(5):
                        line = jnp.broadcast_to(table[5 * p + v : 5 * p + v + 1, :], (8, 128))
                        d.append(jnp.take_along_axis(line, shade, axis=1, mode="promise_in_bounds"))
                        bank[(SEED + 5 * p + v,) + at] = d[v]
                    dvel = [(d[1 + e] - vel[e] * d[0]) * r for e in range(3)]
                    dpress = 0.4 * (d[4] - (vel[0] * d[1] + vel[1] * d[2] + vel[2] * d[3]) + half * d[0])
                    dheat = (dpress - heat * d[0]) * r
                    for e in range(3):
                        bank[(PRIM + 4 + 4 * p + e,) + at] = dvel[e]
                    bank[(PRIM + 7 + 4 * p,) + at] = dheat
                    warm = 0.7 * dheat
                    dtotal = d[4] + dpress
                    for e in axes:
                        dspeed = (vel[e] * dvel[e] + warm) * inverse[e]
                        fluxes = []
                        for g in range(3):
                            move = d[1 + g] * vel[e] + u[1 + g] * dvel[e]
                            fluxes.append(move + dpress if g == e else move)
                        fluxes.append(dtotal * vel[e] + total * dvel[e])
                        if e == 0:
                            bank[(SPEED + 1 + p,) + at] = dspeed
                        else:
                            speed_yz[(3 * e - 2 + p,) + at] = dspeed
                        for g in range(4):
                            if e == 0:
                                bank[(FLUX + 4 * p + g,) + at] = fluxes[g]
                            else:
                                flux_yz[(8 * e - 8 + 4 * p + g,) + at] = fluxes[g]


def inviscid_yz(bank, speed_yz, flux_yz, cell, face, acc):
    count = acc.shape[3] // 8
    places = [(l, t) for l in range(2) for t in range(count)]
    for l, t in places:
        row = BASE + 8 * t
        for p in range(2):
            for v in range(5):
                if v == 0:
                    f = get(bank, SEED + 5 * p + 2, l, row)
                else:
                    f = get(flux_yz, 4 * p + v - 1, l, row)
                put(cell, 5 * p + v, l, 8 * t, (8.0 / 12.0) * f - (1.0 / 12.0) * (ahead(f) + ahead(f, -1)))
    for l, t in places:
        row = BASE + 8 * t
        here = get(speed_yz, 0, l, row)
        s_sum = here + ahead(here)
        ds = []
        for p in range(2):
            here = get(speed_yz, 1 + p, l, row)
            ds.append(here + ahead(here))
        for v in range(5):
            here = get(bank, STATE + v, l, row)
            jump = ahead(here) - here
            for p in range(2):
                here = get(bank, SEED + 5 * p + v, l, row)
                central = get(cell, 5 * p + v, l, 8 * t)
                made = ds[p] * jump + s_sum * (ahead(here) - here) - (central + ahead(central))
                put(face, 5 * p + v, l, 8 * t, made)
    for t in range(count):
        row = BASE + 8 * t
        s_sum = get(speed_yz, 3, 0, row) + get(speed_yz, 3, 1, row)
        ds = [get(speed_yz, 4 + p, 0, row) + get(speed_yz, 4 + p, 1, row) for p in range(2)]
        for v in range(5):
            jump = get(bank, STATE + v, 1, row) - get(bank, STATE + v, 0, row)
            for p in range(2):
                if v == 0:
                    mean = get(bank, SEED + 5 * p + 3, 0, row) + get(bank, SEED + 5 * p + 3, 1, row)
                else:
                    mean = get(flux_yz, 8 + 4 * p + v - 1, 0, row) + get(flux_yz, 8 + 4 * p + v - 1, 1, row)
                djump = get(bank, SEED + 5 * p + v, 1, row) - get(bank, SEED + 5 * p + v, 0, row)
                wall = 0.5 * mean - (ds[p] * jump + s_sum * djump)
                for l in range(2):
                    made = get(face, 5 * p + v, l, 8 * t)
                    made = made - ahead(made, -1)
                    put(acc, 5 * p + v, l, 8 * t, made + wall if l == 1 else made - wall)


def stresses(bank, stress, rows):
    quarter = 0.25 * MU
    for row in rows:
        for k in range(3):
            q = PRIM + 4 * k
            grad_z = [2.0 * (get(bank, q + i, 1, row) - get(bank, q + i, 0, row)) for i in range(4 if k else 3)]
            for l in range(2):
                count = range(4 if k else 3)
                grad_x = [get(bank, q + i, l, row + 1) - get(bank, q + i, l, row - 1) for i in count]
                here = [get(bank, q + i, l, row) for i in count]
                grad_y = [ahead(h, 1) - ahead(h, -1) for h in here]
                third = (2.0 / 3.0) * (grad_x[0] + grad_y[1] + grad_z[2])
                base = 9 * k - 3 if k else 0
                put(stress, base, l, row, quarter * (2.0 * grad_x[0] - third))
                put(stress, base + 1, l, row, quarter * (grad_y[0] + grad_x[1]))
                put(stress, base + 2, l, row, quarter * (grad_z[0] + grad_x[2]))
                put(stress, base + 3, l, row, quarter * (2.0 * grad_y[1] - third))
                put(stress, base + 4, l, row, quarter * (grad_z[1] + grad_y[2]))
                put(stress, base + 5, l, row, quarter * (2.0 * grad_z[2] - third))
                if k > 0:
                    put(stress, base + 6, l, row, (0.25 * KAPPA) * grad_x[3])
                    put(stress, base + 7, l, row, (0.25 * KAPPA) * grad_y[3])
                    put(stress, base + 8, l, row, (0.25 * KAPPA) * grad_z[3])


def x_faces(bank, stress, xface, rows):
    for l in range(2):
        for row in rows:
            pair = lambda ref, f: get(ref, f, l, row) + get(ref, f, l, row + 1)
            s_sum = pair(bank, SPEED)
            ds = [pair(bank, SPEED + 1 + p) for p in range(2)]
            for v in range(5):
                jump = get(bank, STATE + v, l, row + 1) - get(bank, STATE + v, l, row)
                for p in range(2):
                    f = SEED + 5 * p + v
                    made = ds[p] * jump + s_sum * (get(bank, f, l, row + 1) - get(bank, f, l, row))
                    if v == 4:
                        work = 0.0
                        for e in range(3):
                            i = TENSOR[0][e]
                            work = work + pair(bank, PRIM + e) * pair(stress, 6 + 9 * p + i)
                            work = work + pair(bank, PRIM + 4 + 4 * p + e) * pair(stress, i)
                        made = made + 0.5 * work
                    put(xface, 5 * p + v, l, row, made)


def finish(bank, stress, xface, yface, ypart, zface, acc, flags, emit):
    count = acc.shape[3] // 8
    for t in range(count):
        row = BASE + 8 * t
        for l in range(2):
            def pair(ref, f):
                here = get(ref, f, l, row)
                return here + ahead(here)

            v_sum = [pair(bank, PRIM + e) for e in range(3)]
            t_sum = [pair(stress, i) for i in TENSOR[1]]
            for p in range(2):
                work = 0.0
                for e in range(3):
                    here = get(stress, 6 + 9 * p + TENSOR[1][e], l, row)
                    after = ahead(here)
                    put(ypart, 4 * p + e, l, 8 * t, after - ahead(here, -1))
                    work = work + v_sum[e] * (here + after)
                    work = work + pair(bank, PRIM + 4 + 4 * p + e) * t_sum[e]
                put(yface, p, l, 8 * t, 0.5 * work)
        both = lambda ref, f: get(ref, f, 0, row) + get(ref, f, 1, row)
        v_sum = [both(bank, PRIM + e) for e in range(3)]
        t_sum = [both(stress, i) for i in TENSOR[2]]
        for p in range(2):
            work = 0.0
            for e in range(3):
                dt = both(stress, 6 + 9 * p + TENSOR[2][e])
                put(zface, 4 * p + e, 0, 8 * t, dt)
                work = work + v_sum[e] * dt + both(bank, PRIM + 4 + 4 * p + e) * t_sum[e]
            put(zface, 4 * p + 3, 0, 8 * t, 0.5 * work + both(stress, 6 + 9 * p + 8))
    for t in range(count):
        for l in range(2):
            for p in range(2):
                here = get(stress, 13 + 9 * p, l, BASE + 8 * t)
                work = get(yface, p, l, 8 * t)
                put(ypart, 4 * p + 3, l, 8 * t, ahead(here) + work - ahead(here + work, -1))
    solid = [flags(8 * t) == 1 for t in range(count)]
    for p in range(2):
        for v in range(5):
            for l in range(2):
                for t in range(count):
                    row = BASE + 8 * t
                    f = SEED + 5 * p + 1 if v == 0 else FLUX + 4 * p + v - 1
                    near = get(bank, f, l, row + 1) - get(bank, f, l, row - 1)
                    far = get(bank, f, l, row + 2) - get(bank, f, l, row - 2)
                    face = get(xface, 5 * p + v, l, row) - get(xface, 5 * p + v, l, row - 1)
                    total = get(acc, 5 * p + v, l, 8 * t) + face - (8.0 / 12.0) * near + (1.0 / 12.0) * far
                    if v > 0:
                        f = 6 + 9 * p + (6 if v == 4 else TENSOR[0][v - 1])
                        viscous = get(stress, f, l, row + 1) - get(stress, f, l, row - 1)
                        viscous = viscous + get(ypart, 4 * p + v - 1, l, 8 * t)
                        wall = get(zface, 4 * p + v - 1, 0, 8 * t)
                        total = total + (viscous + wall if l == 0 else viscous - wall)
                    value = jnp.where(solid[t], -get(bank, SEED + 5 * p + v, l, row), total)
                    emit(5 * p + v, l, 8 * t, value)


def pack_x(flow, colour, flags, weights, to_near, to_far, flow_out, colour_out, flags_out, weights_out, sems):
    pairs = ((flow, flow_out), (colour, colour_out), (flags, flags_out), (weights, weights_out))
    copies = [pltpu.make_async_copy(src, dst, sems.at[i]) for i, (src, dst) in enumerate(pairs)]
    for copy in copies:
        copy.start()
    for copy in copies:
        copy.wait()
    odd = lax.rem(lax.axis_index("gx"), 2)

    def fill(dst, start):
        for l in range(2):
            for v in range(5):
                dst[4 * v + 2 * l : 4 * v + 2 * l + 2, :] = flow_out[v, l, start : start + 2, :]
            dst[20 + 2 * l : 22 + 2 * l, :] = colour_out[l, start : start + 2, :].astype(jnp.float32)

    @pl.when(odd == 0)
    def _():
        fill(to_near, 14)
        fill(to_far, 0)

    @pl.when(odd == 1)
    def _():
        fill(to_near, 0)
        fill(to_far, 14)


def own_cells(
    flow, colour, weights, flags, acc, table, result, bank, speed_yz, flux_yz, cell, face, stress, xface, yface, ypart,
    zface,
):
    for p in range(2):
        for v in range(5):
            line = weights[v, p : p + 1, :]
            table[5 * p + v : 5 * p + v + 1, :] = jnp.concatenate([line, jnp.zeros((1, 101), jnp.float32)], axis=1)
    for l in range(2):
        for c in range(4):
            lanes = slice(128 * c, 128 * c + 128)
            for v in range(5):
                bank[STATE + v, l, c, BASE : BASE + 16, :] = flow[v, l, :, lanes]
            bank[STATE + 5, l, c, BASE : BASE + 16, :] = colour[l, :, lanes].astype(jnp.float32)
    pointwise(bank, table, (BASE, BASE + 8), speed_yz, flux_yz)
    inviscid_yz(bank, speed_yz, flux_yz, cell, face, acc)
    stresses(bank, stress, (BASE, BASE + 8))
    x_faces(bank, stress, xface, (BASE, BASE + 8))
    solid = lambda row: flags[row : row + 8, :]
    emit = lambda f, l, row, value: put(result, f, l, row, value)
    finish(bank, stress, xface, yface, ypart, zface, acc, solid, emit)


def x_halo(near, far, store, above=BASE + 16):
    odd = lax.rem(lax.axis_index("gx"), 2)

    def fill(src, row):
        for l in range(2):
            for v in range(6):
                store(v, l, row, src, 4 * v + 2 * l)

    @pl.when(odd == 0)
    def _():
        fill(far, BASE - 2)
        fill(near, above)

    @pl.when(odd == 1)
    def _():
        fill(near, BASE - 2)
        fill(far, above)


def pack_y(flow, colour, near, far, table, edge, to_far, to_near):
    for l in range(2):
        for side in range(2):
            lanes = slice(384 * side, 384 * side + 128)
            for v in range(5):
                edge[v, l, side, BASE : BASE + 16, :] = flow[v, l, :, lanes]
            edge[5, l, side, BASE : BASE + 16, :] = colour[l, :, lanes].astype(jnp.float32)

    def store(v, l, row, src, at):
        for side in range(2):
            edge[v, l, side, row : row + 2, :] = src[at : at + 2, 384 * side : 384 * side + 128]

    x_halo(near, far, store)
    lane = lax.broadcasted_iota(jnp.int32, (24, 128), 1)

    def columns(side, first):
        made = jnp.zeros((24, 128), jnp.float32)
        for l in range(2):
            for v in range(6):
                at = 2 * (6 * l + v)
                moved = pltpu.roll(edge[v, l, side, BASE - 4 : BASE + 20, :], (at - first) % 128, 1)
                made = jnp.where((lane >= at) & (lane < at + 2), moved, made)
        return made

    left, right = columns(0, 0), columns(1, 126)
    odd = lax.rem(lax.axis_index("gy"), 2)

    @pl.when(odd == 0)
    def _():
        to_near[...] = right
        to_far[...] = left

    @pl.when(odd == 1)
    def _():
        to_near[...] = left
        to_far[...] = right


def edge_rows(
    near, far, flow, colour, table, flags, whole, result_in, result, bank, acc, stress, xface, yface, ypart, zface
):
    for l in range(2):
        for c in range(4):
            lanes = slice(128 * c, 128 * c + 128)
            for first, row in ((0, BASE), (12, BASE + 4)):
                for v in range(5):
                    bank[STATE + v, l, c, row : row + 4, :] = flow[v, l, first : first + 4, lanes]
                bank[STATE + 5, l, c, row : row + 4, :] = colour[l, first : first + 4, lanes].astype(jnp.float32)

    def store(v, l, row, src, at):
        for c in range(4):
            bank[STATE + v, l, c, row : row + 2, :] = src[at : at + 2, 128 * c : 128 * c + 128]

    x_halo(near, far, store, BASE + 8)
    rows = (BASE - 4, BASE + 4)
    pointwise(bank, table, rows)
    stresses(bank, stress, rows)
    x_faces(bank, stress, xface, rows)
    upper = lax.broadcasted_iota(jnp.int32, (8, 512), 0) < 4
    for f in range(10):
        for l in range(2):
            put(acc, f, l, 0, jnp.where(upper, get(whole, f, l, 0), get(whole, f, l, 8)))

    def emit(f, l, row, made):
        for c in range(4):
            lanes = slice(128 * c, 128 * c + 128)
            result[f, l, c, 0:2, :] = made[0:2, lanes]
            result[f, l, c, 14:16, :] = made[6:8, lanes]

    solid = lambda row: jnp.where(upper, flags[0:8, :], flags[8:16, :])
    finish(bank, stress, xface, yface, ypart, zface, acc, solid, emit)


def edge_columns(
    far, near, edge, table, flags, result, out, bank, acc, speed_yz, flux_yz, cell, face, stress, xface, yface, ypart,
    zface, staged, middle_sem, edge_sem,
):
    middle = []
    for c in (1, 2):
        lanes = slice(128 * c, 128 * c + 128)
        middle.append(pltpu.make_async_copy(result.at[:, :, c], out.at[:, :, :, lanes], middle_sem.at[c - 1]))
        middle[-1].start()
    lane = lax.broadcasted_iota(jnp.int32, (24, 128), 1)
    odd = lax.rem(lax.axis_index("gy"), 2)

    def unpack(low, high):
        for l in range(2):
            for v in range(6):
                at = 2 * (6 * l + v)
                first = edge[v, l, 0, BASE - 4 : BASE + 20, :]
                last = pltpu.roll(edge[v, l, 1, BASE - 4 : BASE + 20, :], 64, 1)
                below = pltpu.roll(low[...], (126 - at) % 128, 1)
                above = pltpu.roll(high[...], 64 - at, 1)
                made = jnp.where(lane < 32, first, last)
                made = jnp.where(lane >= 64, above, made)
                bank[STATE + v, l, 0, BASE - 4 : BASE + 20, :] = jnp.where(lane >= 96, below, made)

    @pl.when(odd == 0)
    def _():
        unpack(far, near)

    @pl.when(odd == 1)
    def _():
        unpack(near, far)

    rows = (BASE - 4, BASE + 4, BASE + 12)
    pointwise(bank, table, rows, speed_yz, flux_yz)
    inviscid_yz(bank, speed_yz, flux_yz, cell, face, acc)
    stresses(bank, stress, rows)
    x_faces(bank, stress, xface, rows)
    column = lax.broadcasted_iota(jnp.int32, (8, 128), 1)

    def solid(row):
        last = pltpu.roll(flags[row : row + 8, 384:512], 64, 1)
        return jnp.where(column < 32, flags[row : row + 8, 0:128], last)

    copies = []

    def emit(f, l, row, made):
        rows = slice(row, row + 8)
        staged[0, f, l, rows, :] = jnp.where(column < 2, made, result[f, l, 0, rows, :])
        staged[1, f, l, rows, :] = jnp.where(column >= 126, pltpu.roll(made, 64, 1), result[f, l, 3, rows, :])
        if l == 1 and row == 8:
            for side in range(2):
                lanes = slice(384 * side, 384 * side + 128)
                copies.append(pltpu.make_async_copy(staged.at[side, f], out.at[f, :, :, lanes], edge_sem.at[side, f]))
                copies[-1].start()

    finish(bank, stress, xface, yface, ypart, zface, acc, solid, emit)
    for copy in middle + copies:
        copy.wait()


def swap(value, axis, offset):
    count = lax.axis_size(axis)
    pairs = []
    for k in range(0, count, 2):
        i, j = (k + offset) % count, (k + offset + 1) % count
        pairs += [(i, j), (j, i)]
    return lax.ppermute(value, axis, pairs)


def local(flow_state, colour_map, cell_flags, probe_weights):
    f32 = jnp.float32
    vmem = pl.BlockSpec(memory_space=pltpu.VMEM)
    hbm = pl.BlockSpec(memory_space=pltpu.HBM)

    def call(kernel, ins, outs, scratch=(), alias={}, cost=0):
        return pl.pallas_call(
            kernel,
            out_shape=[jax.ShapeDtypeStruct(s, d) for s, d, _ in outs],
            in_specs=ins,
            out_specs=[m for _, _, m in outs],
            scratch_shapes=scratch,
            input_output_aliases=alias,
            compiler_params=pltpu.CompilerParams(vmem_limit_bytes=24 * 1024 * 1024),
            cost_estimate=pl.CostEstimate(flops=cost, bytes_accessed=cost, transcendentals=0),
        )

    def banks(n, tiles, rows=ROWS):
        return pltpu.VMEM((n, 2, tiles, rows, 128), f32)

    inputs = [flow_state, colour_map, cell_flags, jnp.transpose(probe_weights, (2, 0, 1))]
    x_near, x_far, flow, colour, flags, weights = call(
        pack_x,
        [hbm] * 4,
        [((24, 512), f32, vmem)] * 2 + [(x.shape, x.dtype, vmem) for x in inputs],
        [pltpu.SemaphoreType.DMA((4,))],
    )(*[pltpu.with_memory_space_constraint(x, pltpu.HBM) for x in inputs])
    x_far = swap(x_far, "gx", 1)
    x_near = swap(x_near, "gx", 0)
    plane = (10, 2, 4, 16, 128)
    acc, table, result = call(
        own_cells,
        [vmem] * 4,
        [(plane, f32, vmem), ((16, 128), f32, vmem), (plane, f32, vmem)],
        [
            banks(FIELDS, 4),
            banks(6, 4),
            banks(16, 4),
            banks(10, 4, 16),
            banks(10, 4, 16),
            banks(24, 4),
            banks(10, 4),
            banks(2, 4, 16),
            banks(8, 4, 16),
            pltpu.VMEM((8, 1, 4, 16, 128), f32),
        ],
        cost=8000000,
    )(flow, colour, weights, flags)
    edge, y_far, y_near = call(
        pack_y,
        [vmem] * 5,
        [((6, 2, 2, ROWS, 128), f32, vmem), ((24, 128), f32, vmem), ((24, 128), f32, vmem)],
    )(flow, colour, x_near, x_far, table)
    y_far = swap(y_far, "gy", 1)
    y_near = swap(y_near, "gy", 0)
    (result,) = call(
        edge_rows,
        [vmem] * 8,
        [(plane, f32, vmem)],
        [
            banks(FIELDS, 4),
            banks(10, 4, 8),
            banks(24, 4),
            banks(10, 4),
            banks(2, 4, 8),
            banks(8, 4, 8),
            pltpu.VMEM((8, 1, 4, 8, 128), f32),
        ],
        alias={7: 0},
        cost=8000000,
    )(x_near, x_far, flow, colour, table, flags, acc, result)
    (out,) = call(
        edge_columns,
        [vmem] * 6,
        [((10, 2, 16, 512), f32, hbm)],
        [
            banks(FIELDS, 1),
            banks(10, 1, 16),
            banks(6, 1),
            banks(16, 1),
            banks(10, 1, 16),
            banks(10, 1, 16),
            banks(24, 1),
            banks(10, 1),
            banks(2, 1, 16),
            banks(8, 1, 16),
            pltpu.VMEM((8, 1, 1, 16, 128), f32),
            pltpu.VMEM((2, 10, 2, 16, 128), f32),
            pltpu.SemaphoreType.DMA((2,)),
            pltpu.SemaphoreType.DMA((2, 10)),
        ],
    )(y_far, y_near, edge, table, flags, result)
    return out.reshape(2, 5, 2, 16, 512)


def solution(mesh):
    return jax.shard_map(
        local,
        mesh=mesh,
        in_specs=(P(None, None, "gx", "gy"), P(None, "gx", "gy"), P("gx", "gy"), P()),
        out_specs=P(None, None, None, "gx", "gy"),
        check_vma=False,
    )
```

```python
import jax
import jax.numpy as jnp
from jax import lax
from jax.experimental import pallas as pl
from jax.experimental.pallas import tpu as pltpu
from jax.sharding import PartitionSpec as P

MU = 0.2
KAPPA = 0.2 * 1.4 / (0.4 * 0.72)
BASE = 12
ROWS = 40
STATE, SEED, PRIM, SPEED, FLUX, FIELDS = 0, 6, 16, 28, 31, 39
TENSOR = ((0, 1, 2), (1, 3, 4), (2, 4, 5))


def get(ref, f, l, row):
    tiles = [ref[f, l, c, row : row + 8, :] for c in range(ref.shape[2])]
    return tiles[0] if len(tiles) == 1 else jnp.concatenate(tiles, axis=1)


def put(ref, f, l, row, value):
    for c in range(ref.shape[2]):
        ref[f, l, c, row : row + 8, :] = value[:, 128 * c : 128 * c + 128]


def ahead(value, step=1):
    return pltpu.roll(value, (-step) % value.shape[1], 1)


def pointwise(bank, table, rows, height, speed_yz=None, flux_yz=None):
    for l in range(2):
        for row in rows:
            for c in range(bank.shape[2]):
                at = (l, c, slice(row, row + height), slice(None))
                u = [bank[(STATE + v,) + at] for v in range(5)]
                shade = bank[(STATE + 5,) + at].astype(jnp.int32) & 127
                r = 1.0 / u[0]
                vel = [u[1 + e] * r for e in range(3)]
                half = 0.5 * (vel[0] * vel[0] + vel[1] * vel[1] + vel[2] * vel[2])
                pressure = 0.4 * (u[4] - half * u[0])
                heat = pressure * r
                total = u[4] + pressure
                for e in range(3):
                    bank[(PRIM + e,) + at] = vel[e]
                bank[(PRIM + 3,) + at] = heat
                axes = range(1 if flux_yz is None else 3)
                inverse = []
                for e in axes:
                    square = vel[e] * vel[e] + 1.4 * heat
                    inv = lax.rsqrt(square)
                    if e == 0:
                        bank[(SPEED,) + at] = 0.25 * (square * inv)
                    else:
                        speed_yz[(3 * e - 3,) + at] = 0.25 * (square * inv)
                    inverse.append(0.25 * inv)
                for p in range(2):
                    d = []
                    for v in range(5):
                        line = jnp.broadcast_to(table[5 * p + v : 5 * p + v + 1, :], (height, 128))
                        d.append(jnp.take_along_axis(line, shade, axis=1, mode="promise_in_bounds"))
                        bank[(SEED + 5 * p + v,) + at] = d[v]
                    dvel = [(d[1 + e] - vel[e] * d[0]) * r for e in range(3)]
                    dpress = 0.4 * (d[4] - (vel[0] * d[1] + vel[1] * d[2] + vel[2] * d[3]) + half * d[0])
                    dheat = (dpress - heat * d[0]) * r
                    for e in range(3):
                        bank[(PRIM + 4 + 4 * p + e,) + at] = dvel[e]
                    bank[(PRIM + 7 + 4 * p,) + at] = dheat
                    warm = 0.7 * dheat
                    dtotal = d[4] + dpress
                    for e in axes:
                        dspeed = (vel[e] * dvel[e] + warm) * inverse[e]
                        fluxes = []
                        for g in range(3):
                            move = d[1 + g] * vel[e] + u[1 + g] * dvel[e]
                            fluxes.append(move + dpress if g == e else move)
                        fluxes.append(dtotal * vel[e] + total * dvel[e])
                        if e == 0:
                            bank[(SPEED + 1 + p,) + at] = dspeed
                        else:
                            speed_yz[(3 * e - 2 + p,) + at] = dspeed
                        for g in range(4):
                            if e == 0:
                                bank[(FLUX + 4 * p + g,) + at] = fluxes[g]
                            else:
                                flux_yz[(8 * e - 8 + 4 * p + g,) + at] = fluxes[g]


def inviscid_yz(bank, speed_yz, flux_yz, cell, face, acc):
    count = acc.shape[3] // 8
    places = [(l, t) for l in range(2) for t in range(count)]
    for l, t in places:
        row = BASE + 8 * t
        for p in range(2):
            for v in range(5):
                if v == 0:
                    f = get(bank, SEED + 5 * p + 2, l, row)
                else:
                    f = get(flux_yz, 4 * p + v - 1, l, row)
                put(cell, 5 * p + v, l, 8 * t, (8.0 / 12.0) * f - (1.0 / 12.0) * (ahead(f) + ahead(f, -1)))
    for l, t in places:
        row = BASE + 8 * t
        here = get(speed_yz, 0, l, row)
        s_sum = here + ahead(here)
        ds = []
        for p in range(2):
            here = get(speed_yz, 1 + p, l, row)
            ds.append(here + ahead(here))
        for v in range(5):
            here = get(bank, STATE + v, l, row)
            jump = ahead(here) - here
            for p in range(2):
                here = get(bank, SEED + 5 * p + v, l, row)
                central = get(cell, 5 * p + v, l, 8 * t)
                made = ds[p] * jump + s_sum * (ahead(here) - here) - (central + ahead(central))
                put(face, 5 * p + v, l, 8 * t, made)
    for t in range(count):
        row = BASE + 8 * t
        s_sum = get(speed_yz, 3, 0, row) + get(speed_yz, 3, 1, row)
        ds = [get(speed_yz, 4 + p, 0, row) + get(speed_yz, 4 + p, 1, row) for p in range(2)]
        for v in range(5):
            jump = get(bank, STATE + v, 1, row) - get(bank, STATE + v, 0, row)
            for p in range(2):
                if v == 0:
                    mean = get(bank, SEED + 5 * p + 3, 0, row) + get(bank, SEED + 5 * p + 3, 1, row)
                else:
                    mean = get(flux_yz, 8 + 4 * p + v - 1, 0, row) + get(flux_yz, 8 + 4 * p + v - 1, 1, row)
                djump = get(bank, SEED + 5 * p + v, 1, row) - get(bank, SEED + 5 * p + v, 0, row)
                wall = 0.5 * mean - (ds[p] * jump + s_sum * djump)
                for l in range(2):
                    made = get(face, 5 * p + v, l, 8 * t)
                    made = made - ahead(made, -1)
                    put(acc, 5 * p + v, l, 8 * t, made + wall if l == 1 else made - wall)


def stresses(bank, stress, rows):
    quarter = 0.25 * MU
    for row in rows:
        for k in range(3):
            q = PRIM + 4 * k
            grad_z = [2.0 * (get(bank, q + i, 1, row) - get(bank, q + i, 0, row)) for i in range(4 if k else 3)]
            for l in range(2):
                count = range(4 if k else 3)
                grad_x = [get(bank, q + i, l, row + 1) - get(bank, q + i, l, row - 1) for i in count]
                here = [get(bank, q + i, l, row) for i in count]
                grad_y = [ahead(h, 1) - ahead(h, -1) for h in here]
                third = (2.0 / 3.0) * (grad_x[0] + grad_y[1] + grad_z[2])
                base = 9 * k - 3 if k else 0
                put(stress, base, l, row, quarter * (2.0 * grad_x[0] - third))
                put(stress, base + 1, l, row, quarter * (grad_y[0] + grad_x[1]))
                put(stress, base + 2, l, row, quarter * (grad_z[0] + grad_x[2]))
                put(stress, base + 3, l, row, quarter * (2.0 * grad_y[1] - third))
                put(stress, base + 4, l, row, quarter * (grad_z[1] + grad_y[2]))
                put(stress, base + 5, l, row, quarter * (2.0 * grad_z[2] - third))
                if k > 0:
                    put(stress, base + 6, l, row, (0.25 * KAPPA) * grad_x[3])
                    put(stress, base + 7, l, row, (0.25 * KAPPA) * grad_y[3])
                    put(stress, base + 8, l, row, (0.25 * KAPPA) * grad_z[3])


def x_faces(bank, stress, xface, rows):
    for l in range(2):
        for row in rows:
            pair = lambda ref, f: get(ref, f, l, row) + get(ref, f, l, row + 1)
            s_sum = pair(bank, SPEED)
            ds = [pair(bank, SPEED + 1 + p) for p in range(2)]
            for v in range(5):
                jump = get(bank, STATE + v, l, row + 1) - get(bank, STATE + v, l, row)
                for p in range(2):
                    f = SEED + 5 * p + v
                    made = ds[p] * jump + s_sum * (get(bank, f, l, row + 1) - get(bank, f, l, row))
                    if v == 4:
                        work = 0.0
                        for e in range(3):
                            i = TENSOR[0][e]
                            work = work + pair(bank, PRIM + e) * pair(stress, 6 + 9 * p + i)
                            work = work + pair(bank, PRIM + 4 + 4 * p + e) * pair(stress, i)
                        made = made + 0.5 * work
                    put(xface, 5 * p + v, l, row, made)


def finish(bank, stress, xface, yface, ypart, zface, acc, flags, emit):
    count = acc.shape[3] // 8
    for t in range(count):
        row = BASE + 8 * t
        for l in range(2):
            def pair(ref, f):
                here = get(ref, f, l, row)
                return here + ahead(here)

            v_sum = [pair(bank, PRIM + e) for e in range(3)]
            t_sum = [pair(stress, i) for i in TENSOR[1]]
            for p in range(2):
                work = 0.0
                for e in range(3):
                    here = get(stress, 6 + 9 * p + TENSOR[1][e], l, row)
                    after = ahead(here)
                    put(ypart, 4 * p + e, l, 8 * t, after - ahead(here, -1))
                    work = work + v_sum[e] * (here + after)
                    work = work + pair(bank, PRIM + 4 + 4 * p + e) * t_sum[e]
                put(yface, p, l, 8 * t, 0.5 * work)
        both = lambda ref, f: get(ref, f, 0, row) + get(ref, f, 1, row)
        v_sum = [both(bank, PRIM + e) for e in range(3)]
        t_sum = [both(stress, i) for i in TENSOR[2]]
        for p in range(2):
            work = 0.0
            for e in range(3):
                dt = both(stress, 6 + 9 * p + TENSOR[2][e])
                put(zface, 4 * p + e, 0, 8 * t, dt)
                work = work + v_sum[e] * dt + both(bank, PRIM + 4 + 4 * p + e) * t_sum[e]
            put(zface, 4 * p + 3, 0, 8 * t, 0.5 * work + both(stress, 6 + 9 * p + 8))
    for t in range(count):
        for l in range(2):
            for p in range(2):
                here = get(stress, 13 + 9 * p, l, BASE + 8 * t)
                work = get(yface, p, l, 8 * t)
                put(ypart, 4 * p + 3, l, 8 * t, ahead(here) + work - ahead(here + work, -1))
    solid = [flags(8 * t) == 1 for t in range(count)]
    for p in range(2):
        for v in range(5):
            for l in range(2):
                for t in range(count):
                    row = BASE + 8 * t
                    f = SEED + 5 * p + 1 if v == 0 else FLUX + 4 * p + v - 1
                    near = get(bank, f, l, row + 1) - get(bank, f, l, row - 1)
                    far = get(bank, f, l, row + 2) - get(bank, f, l, row - 2)
                    face = get(xface, 5 * p + v, l, row) - get(xface, 5 * p + v, l, row - 1)
                    total = get(acc, 5 * p + v, l, 8 * t) + face - (8.0 / 12.0) * near + (1.0 / 12.0) * far
                    if v > 0:
                        f = 6 + 9 * p + (6 if v == 4 else TENSOR[0][v - 1])
                        viscous = get(stress, f, l, row + 1) - get(stress, f, l, row - 1)
                        viscous = viscous + get(ypart, 4 * p + v - 1, l, 8 * t)
                        wall = get(zface, 4 * p + v - 1, 0, 8 * t)
                        total = total + (viscous + wall if l == 0 else viscous - wall)
                    value = jnp.where(solid[t], -get(bank, SEED + 5 * p + v, l, row), total)
                    emit(5 * p + v, l, 8 * t, value)


def pack_x(flow, colour, flags, weights, to_near, to_far, flow_out, colour_out, flags_out, weights_out, sems):
    pairs = ((flow, flow_out), (colour, colour_out), (flags, flags_out), (weights, weights_out))
    copies = [pltpu.make_async_copy(src, dst, sems.at[i]) for i, (src, dst) in enumerate(pairs)]
    for copy in copies:
        copy.start()
    for copy in copies:
        copy.wait()
    odd = lax.rem(lax.axis_index("gx"), 2)

    def fill(dst, start):
        for l in range(2):
            for v in range(5):
                dst[4 * v + 2 * l : 4 * v + 2 * l + 2, :] = flow_out[v, l, start : start + 2, :]
            dst[20 + 2 * l : 22 + 2 * l, :] = colour_out[l, start : start + 2, :].astype(jnp.float32)

    @pl.when(odd == 0)
    def _():
        fill(to_near, 14)
        fill(to_far, 0)

    @pl.when(odd == 1)
    def _():
        fill(to_near, 0)
        fill(to_far, 14)


def own_cells(flow, colour, weights, bank, acc, table, speed_yz, flux_yz, cell, face):
    for p in range(2):
        for v in range(5):
            line = weights[v, p : p + 1, :]
            table[5 * p + v : 5 * p + v + 1, :] = jnp.concatenate([line, jnp.zeros((1, 101), jnp.float32)], axis=1)
    for l in range(2):
        for c in range(4):
            lanes = slice(128 * c, 128 * c + 128)
            for v in range(5):
                bank[STATE + v, l, c, BASE : BASE + 16, :] = flow[v, l, :, lanes]
            bank[STATE + 5, l, c, BASE : BASE + 16, :] = colour[l, :, lanes].astype(jnp.float32)
    pointwise(bank, table, (BASE, BASE + 8), 8, speed_yz, flux_yz)
    inviscid_yz(bank, speed_yz, flux_yz, cell, face, acc)


def x_halo(near, far, store):
    odd = lax.rem(lax.axis_index("gx"), 2)

    def fill(src, row):
        for l in range(2):
            for v in range(6):
                store(v, l, row, src, 4 * v + 2 * l)

    @pl.when(odd == 0)
    def _():
        fill(far, BASE - 2)
        fill(near, BASE + 16)

    @pl.when(odd == 1)
    def _():
        fill(near, BASE - 2)
        fill(far, BASE + 16)


def fold(first, last):
    rows = first.shape[0] - 8
    lane = lax.broadcasted_iota(jnp.int32, first.shape, 1)
    made = jnp.where(lane < 64, pltpu.roll(first, 32, 1), last)
    return jnp.where((lane[:rows] >= 48) & (lane[:rows] < 112), pltpu.roll(made[8:], 64, 1), made[:rows])


def pack_y(flow, colour, near, far, table, strip, to_far, to_near, edge):
    for l in range(2):
        for side in range(2):
            lanes = slice(384 * side, 384 * side + 128)
            for v in range(5):
                edge[v, l, side, BASE : BASE + 16, :] = flow[v, l, :, lanes]
            edge[5, l, side, BASE : BASE + 16, :] = colour[l, :, lanes].astype(jnp.float32)

    def store(v, l, row, src, at):
        for side in range(2):
            edge[v, l, side, row : row + 2, :] = src[at : at + 2, 384 * side : 384 * side + 128]

    x_halo(near, far, store)
    lane = lax.broadcasted_iota(jnp.int32, (24, 128), 1)

    def columns(side, first):
        made = jnp.zeros((24, 128), jnp.float32)
        for l in range(2):
            for v in range(6):
                at = 2 * (6 * l + v)
                moved = pltpu.roll(edge[v, l, side, BASE - 4 : BASE + 20, :], (at - first) % 128, 1)
                made = jnp.where((lane >= at) & (lane < at + 2), moved, made)
        return jnp.where(lane[:16] < 64, made[:16], pltpu.roll(made[8:], 64, 1))

    for v in range(6):
        for l in range(2):
            span = slice(BASE - 4, BASE + 20)
            strip[v, l] = fold(edge[v, l, 0, span, :], edge[v, l, 1, span, :])
    left, right = columns(0, 0), columns(1, 126)
    odd = lax.rem(lax.axis_index("gy"), 2)

    @pl.when(odd == 0)
    def _():
        to_near[...] = right
        to_far[...] = left

    @pl.when(odd == 1)
    def _():
        to_near[...] = left
        to_far[...] = right


def whole_rows(near, far, table, flags, bank_in, acc, bank, result, stress, xface, yface, ypart, zface):
    def store(v, l, row, src, at):
        for c in range(4):
            bank[STATE + v, l, c, row : row + 2, :] = src[at : at + 2, 128 * c : 128 * c + 128]

    x_halo(near, far, store)
    pointwise(bank, table, (BASE - 4, BASE + 12), 8)
    rows = (BASE - 4, BASE + 4, BASE + 12)
    stresses(bank, stress, rows)
    x_faces(bank, stress, xface, rows)
    solid = lambda row: flags[row : row + 8, :]
    emit = lambda f, l, row, value: put(result, f, l, row, value)
    finish(bank, stress, xface, yface, ypart, zface, acc, solid, emit)


def edge_columns(
    far, near, strip, table, flags, result, out, bank, acc, speed_yz, flux_yz, cell, face, stress, xface, yface, ypart,
    zface, staged, middle_sem, edge_sem,
):
    middle = []
    for c in (1, 2):
        lanes = slice(128 * c, 128 * c + 128)
        middle.append(pltpu.make_async_copy(result.at[:, :, c], out.at[:, :, :, lanes], middle_sem.at[c - 1]))
        middle[-1].start()
    lane = lax.broadcasted_iota(jnp.int32, (16, 128), 1)
    place = lane & 63
    odd = lax.rem(lax.axis_index("gy"), 2)

    def unpack(low, high):
        for l in range(2):
            for v in range(6):
                at = 2 * (6 * l + v)
                made = jnp.where(place < 2, pltpu.roll(high[...], (-at) % 128, 1), strip[v, l])
                made = jnp.where((place == 30) | (place == 31), pltpu.roll(low[...], 30 - at, 1), made)
                bank[STATE + v, l, 0, BASE - 4 : BASE + 12, :] = made

    @pl.when(odd == 0)
    def _():
        unpack(far, near)

    @pl.when(odd == 1)
    def _():
        unpack(near, far)

    rows = (BASE - 4, BASE + 4)
    pointwise(bank, table, (BASE - 4,), 16, speed_yz, flux_yz)
    inviscid_yz(bank, speed_yz, flux_yz, cell, face, acc)
    stresses(bank, stress, rows)
    x_faces(bank, stress, xface, rows)
    column = lane[:8]
    solid = lambda row: fold(flags[:, 0:128], flags[:, 384:512])
    copies = []

    def emit(f, l, row, made):
        top, low = slice(0, 8), slice(8, 16)
        half, rest = pltpu.roll(made, 64, 1), pltpu.roll(made, 32, 1)
        staged[0, f, l, top, :] = jnp.where(column < 2, pltpu.roll(made, 96, 1), result[f, l, 0, top, :])
        staged[0, f, l, low, :] = jnp.where(column < 2, rest, result[f, l, 0, low, :])
        staged[1, f, l, top, :] = jnp.where(column >= 126, made, result[f, l, 3, top, :])
        staged[1, f, l, low, :] = jnp.where(column >= 126, half, result[f, l, 3, low, :])
        if l == 1:
            for side in range(2):
                lanes = slice(384 * side, 384 * side + 128)
                copies.append(pltpu.make_async_copy(staged.at[side, f], out.at[f, :, :, lanes], edge_sem.at[side, f]))
                copies[-1].start()

    finish(bank, stress, xface, yface, ypart, zface, acc, solid, emit)
    for copy in middle + copies:
        copy.wait()


def swap(value, axis, offset):
    count = lax.axis_size(axis)
    pairs = []
    for k in range(0, count, 2):
        i, j = (k + offset) % count, (k + offset + 1) % count
        pairs += [(i, j), (j, i)]
    return lax.ppermute(value, axis, pairs)


def local(flow_state, colour_map, cell_flags, probe_weights):
    f32 = jnp.float32
    vmem = pl.BlockSpec(memory_space=pltpu.VMEM)
    hbm = pl.BlockSpec(memory_space=pltpu.HBM)

    def call(kernel, ins, outs, scratch=(), alias={}, cost=0):
        return pl.pallas_call(
            kernel,
            out_shape=[jax.ShapeDtypeStruct(s, d) for s, d, _ in outs],
            in_specs=ins,
            out_specs=[m for _, _, m in outs],
            scratch_shapes=scratch,
            input_output_aliases=alias,
            compiler_params=pltpu.CompilerParams(vmem_limit_bytes=24 * 1024 * 1024),
            cost_estimate=pl.CostEstimate(flops=cost, bytes_accessed=cost, transcendentals=0),
        )

    def banks(n, tiles, rows=ROWS):
        return pltpu.VMEM((n, 2, tiles, rows, 128), f32)

    inputs = [flow_state, colour_map, cell_flags, jnp.transpose(probe_weights, (2, 0, 1))]
    x_near, x_far, flow, colour, flags, weights = call(
        pack_x,
        [hbm] * 4,
        [((24, 512), f32, vmem)] * 2 + [(x.shape, x.dtype, vmem) for x in inputs],
        [pltpu.SemaphoreType.DMA((4,))],
    )(*[pltpu.with_memory_space_constraint(x, pltpu.HBM) for x in inputs])
    x_far = swap(x_far, "gx", 1)
    x_near = swap(x_near, "gx", 0)
    bank, acc, table = call(
        own_cells,
        [vmem] * 3,
        [((FIELDS, 2, 4, ROWS, 128), f32, vmem), ((10, 2, 4, 16, 128), f32, vmem), ((16, 128), f32, vmem)],
        [banks(6, 4), banks(16, 4), banks(10, 4, 16), banks(10, 4, 16)],
        cost=8000000,
    )(flow, colour, weights)
    strip, y_far, y_near = call(
        pack_y,
        [vmem] * 5,
        [((6, 2, 16, 128), f32, vmem), ((16, 128), f32, vmem), ((16, 128), f32, vmem)],
        [banks(6, 2)],
    )(flow, colour, x_near, x_far, table)
    y_far = swap(y_far, "gy", 1)
    y_near = swap(y_near, "gy", 0)
    bank, result = call(
        whole_rows,
        [vmem] * 6,
        [(bank.shape, f32, vmem), (acc.shape, f32, vmem)],
        [banks(24, 4), banks(10, 4), banks(2, 4, 16), banks(8, 4, 16), pltpu.VMEM((8, 1, 4, 16, 128), f32)],
        alias={4: 0, 5: 1},
        cost=8000000,
    )(x_near, x_far, table, flags, bank, acc)
    (out,) = call(
        edge_columns,
        [vmem] * 6,
        [((10, 2, 16, 512), f32, hbm)],
        [
            banks(FIELDS, 1),
            banks(10, 1, 8),
            banks(6, 1),
            banks(16, 1),
            banks(10, 1, 8),
            banks(10, 1, 8),
            banks(24, 1),
            banks(10, 1),
            banks(2, 1, 8),
            banks(8, 1, 8),
            pltpu.VMEM((8, 1, 1, 8, 128), f32),
            pltpu.VMEM((2, 10, 2, 16, 128), f32),
            pltpu.SemaphoreType.DMA((2,)),
            pltpu.SemaphoreType.DMA((2, 10)),
        ],
    )(y_far, y_near, strip, table, flags, result)
    return out.reshape(2, 5, 2, 16, 512)


def solution(mesh):
    return jax.shard_map(
        local,
        mesh=mesh,
        in_specs=(P(None, None, "gx", "gy"), P(None, "gx", "gy"), P("gx", "gy"), P()),
        out_specs=P(None, None, None, "gx", "gy"),
        check_vma=False,
    )
```

```python
import jax
import jax.numpy as jnp
from jax import lax
from jax.experimental import pallas as pl
from jax.experimental.pallas import tpu as pltpu
from jax.sharding import PartitionSpec as P

MU = 0.2
KAPPA = 0.2 * 1.4 / (0.4 * 0.72)
BASE = 12
ROWS = 40
STATE, SEED, PRIM, SPEED, FLUX, FIELDS = 0, 6, 16, 28, 31, 39
TENSOR = ((0, 1, 2), (1, 3, 4), (2, 4, 5))


def get(ref, f, l, row, height=8):
    tiles = [ref[f, l, c, row : row + height, :] for c in range(ref.shape[2])]
    return tiles[0] if len(tiles) == 1 else jnp.concatenate(tiles, axis=1)


def put(ref, f, l, row, value):
    for c in range(ref.shape[2]):
        ref[f, l, c, row : row + value.shape[0], :] = value[:, 128 * c : 128 * c + 128]


def ahead(value, step=1):
    return pltpu.roll(value, (-step) % value.shape[1], 1)


def pointwise(bank, table, rows, height, speed_yz=None, flux_yz=None):
    for l in range(2):
        for row in rows:
            for c in range(bank.shape[2]):
                at = (l, c, slice(row, row + height), slice(None))
                u = [bank[(STATE + v,) + at] for v in range(5)]
                shade = bank[(STATE + 5,) + at].astype(jnp.int32) & 127
                r = 1.0 / u[0]
                vel = [u[1 + e] * r for e in range(3)]
                half = 0.5 * (vel[0] * vel[0] + vel[1] * vel[1] + vel[2] * vel[2])
                pressure = 0.4 * (u[4] - half * u[0])
                heat = pressure * r
                total = u[4] + pressure
                for e in range(3):
                    bank[(PRIM + e,) + at] = vel[e]
                bank[(PRIM + 3,) + at] = heat
                axes = range(1 if flux_yz is None else 3)
                inverse = []
                for e in axes:
                    square = vel[e] * vel[e] + 1.4 * heat
                    inv = lax.rsqrt(square)
                    if e == 0:
                        bank[(SPEED,) + at] = 0.25 * (square * inv)
                    else:
                        speed_yz[(3 * e - 3,) + at] = 0.25 * (square * inv)
                    inverse.append(0.25 * inv)
                for p in range(2):
                    d = []
                    for v in range(5):
                        line = jnp.broadcast_to(table[5 * p + v : 5 * p + v + 1, :], (height, 128))
                        d.append(jnp.take_along_axis(line, shade, axis=1, mode="promise_in_bounds"))
                        bank[(SEED + 5 * p + v,) + at] = d[v]
                    dvel = [(d[1 + e] - vel[e] * d[0]) * r for e in range(3)]
                    dpress = 0.4 * (d[4] - (vel[0] * d[1] + vel[1] * d[2] + vel[2] * d[3]) + half * d[0])
                    dheat = (dpress - heat * d[0]) * r
                    for e in range(3):
                        bank[(PRIM + 4 + 4 * p + e,) + at] = dvel[e]
                    bank[(PRIM + 7 + 4 * p,) + at] = dheat
                    warm = 0.7 * dheat
                    dtotal = d[4] + dpress
                    for e in axes:
                        dspeed = (vel[e] * dvel[e] + warm) * inverse[e]
                        fluxes = []
                        for g in range(3):
                            move = d[1 + g] * vel[e] + u[1 + g] * dvel[e]
                            fluxes.append(move + dpress if g == e else move)
                        fluxes.append(dtotal * vel[e] + total * dvel[e])
                        if e == 0:
                            bank[(SPEED + 1 + p,) + at] = dspeed
                        else:
                            speed_yz[(3 * e - 2 + p,) + at] = dspeed
                        for g in range(4):
                            if e == 0:
                                bank[(FLUX + 4 * p + g,) + at] = fluxes[g]
                            else:
                                flux_yz[(8 * e - 8 + 4 * p + g,) + at] = fluxes[g]


def inviscid_yz(bank, speed_yz, flux_yz, cell, face, acc):
    count = acc.shape[3] // 8
    places = [(l, t) for l in range(2) for t in range(count)]
    for l, t in places:
        row = BASE + 8 * t
        for p in range(2):
            for v in range(5):
                if v == 0:
                    f = get(bank, SEED + 5 * p + 2, l, row)
                else:
                    f = get(flux_yz, 4 * p + v - 1, l, row)
                put(cell, 5 * p + v, l, 8 * t, (8.0 / 12.0) * f - (1.0 / 12.0) * (ahead(f) + ahead(f, -1)))
    for l, t in places:
        row = BASE + 8 * t
        here = get(speed_yz, 0, l, row)
        s_sum = here + ahead(here)
        ds = []
        for p in range(2):
            here = get(speed_yz, 1 + p, l, row)
            ds.append(here + ahead(here))
        for v in range(5):
            here = get(bank, STATE + v, l, row)
            jump = ahead(here) - here
            for p in range(2):
                here = get(bank, SEED + 5 * p + v, l, row)
                central = get(cell, 5 * p + v, l, 8 * t)
                made = ds[p] * jump + s_sum * (ahead(here) - here) - (central + ahead(central))
                put(face, 5 * p + v, l, 8 * t, made)
    for t in range(count):
        row = BASE + 8 * t
        s_sum = get(speed_yz, 3, 0, row) + get(speed_yz, 3, 1, row)
        ds = [get(speed_yz, 4 + p, 0, row) + get(speed_yz, 4 + p, 1, row) for p in range(2)]
        for v in range(5):
            jump = get(bank, STATE + v, 1, row) - get(bank, STATE + v, 0, row)
            for p in range(2):
                if v == 0:
                    mean = get(bank, SEED + 5 * p + 3, 0, row) + get(bank, SEED + 5 * p + 3, 1, row)
                else:
                    mean = get(flux_yz, 8 + 4 * p + v - 1, 0, row) + get(flux_yz, 8 + 4 * p + v - 1, 1, row)
                djump = get(bank, SEED + 5 * p + v, 1, row) - get(bank, SEED + 5 * p + v, 0, row)
                wall = 0.5 * mean - (ds[p] * jump + s_sum * djump)
                for l in range(2):
                    made = get(face, 5 * p + v, l, 8 * t)
                    made = made - ahead(made, -1)
                    put(acc, 5 * p + v, l, 8 * t, made + wall if l == 1 else made - wall)


def stresses(bank, stress, rows, height=8):
    quarter = 0.25 * MU
    for row in rows:
        for k in range(3):
            q = PRIM + 4 * k
            grad_z = [2.0 * (get(bank, q + i, 1, row, height) - get(bank, q + i, 0, row, height)) for i in range(4 if k else 3)]
            for l in range(2):
                count = range(4 if k else 3)
                grad_x = [get(bank, q + i, l, row + 1, height) - get(bank, q + i, l, row - 1, height) for i in count]
                here = [get(bank, q + i, l, row, height) for i in count]
                grad_y = [ahead(h, 1) - ahead(h, -1) for h in here]
                third = (2.0 / 3.0) * (grad_x[0] + grad_y[1] + grad_z[2])
                base = 9 * k - 3 if k else 0
                put(stress, base, l, row, quarter * (2.0 * grad_x[0] - third))
                put(stress, base + 1, l, row, quarter * (grad_y[0] + grad_x[1]))
                put(stress, base + 2, l, row, quarter * (grad_z[0] + grad_x[2]))
                put(stress, base + 3, l, row, quarter * (2.0 * grad_y[1] - third))
                put(stress, base + 4, l, row, quarter * (grad_z[1] + grad_y[2]))
                put(stress, base + 5, l, row, quarter * (2.0 * grad_z[2] - third))
                if k > 0:
                    put(stress, base + 6, l, row, (0.25 * KAPPA) * grad_x[3])
                    put(stress, base + 7, l, row, (0.25 * KAPPA) * grad_y[3])
                    put(stress, base + 8, l, row, (0.25 * KAPPA) * grad_z[3])


def x_faces(bank, stress, xface, rows, height=8):
    for l in range(2):
        for row in rows:
            pair = lambda ref, f: get(ref, f, l, row, height) + get(ref, f, l, row + 1, height)
            s_sum = pair(bank, SPEED)
            ds = [pair(bank, SPEED + 1 + p) for p in range(2)]
            for v in range(5):
                jump = get(bank, STATE + v, l, row + 1, height) - get(bank, STATE + v, l, row, height)
                for p in range(2):
                    f = SEED + 5 * p + v
                    made = ds[p] * jump + s_sum * (get(bank, f, l, row + 1, height) - get(bank, f, l, row, height))
                    if v == 4:
                        work = 0.0
                        for e in range(3):
                            i = TENSOR[0][e]
                            work = work + pair(bank, PRIM + e) * pair(stress, 6 + 9 * p + i)
                            work = work + pair(bank, PRIM + 4 + 4 * p + e) * pair(stress, i)
                        made = made + 0.5 * work
                    put(xface, 5 * p + v, l, row, made)


def finish(bank, stress, xface, yface, ypart, zface, acc, flags, emit):
    count = acc.shape[3] // 8
    for t in range(count):
        row = BASE + 8 * t
        for l in range(2):
            def pair(ref, f):
                here = get(ref, f, l, row)
                return here + ahead(here)

            v_sum = [pair(bank, PRIM + e) for e in range(3)]
            t_sum = [pair(stress, i) for i in TENSOR[1]]
            for p in range(2):
                work = 0.0
                for e in range(3):
                    here = get(stress, 6 + 9 * p + TENSOR[1][e], l, row)
                    after = ahead(here)
                    put(ypart, 4 * p + e, l, 8 * t, after - ahead(here, -1))
                    work = work + v_sum[e] * (here + after)
                    work = work + pair(bank, PRIM + 4 + 4 * p + e) * t_sum[e]
                put(yface, p, l, 8 * t, 0.5 * work)
        both = lambda ref, f: get(ref, f, 0, row) + get(ref, f, 1, row)
        v_sum = [both(bank, PRIM + e) for e in range(3)]
        t_sum = [both(stress, i) for i in TENSOR[2]]
        for p in range(2):
            work = 0.0
            for e in range(3):
                dt = both(stress, 6 + 9 * p + TENSOR[2][e])
                put(zface, 4 * p + e, 0, 8 * t, dt)
                work = work + v_sum[e] * dt + both(bank, PRIM + 4 + 4 * p + e) * t_sum[e]
            put(zface, 4 * p + 3, 0, 8 * t, 0.5 * work + both(stress, 6 + 9 * p + 8))
    for t in range(count):
        for l in range(2):
            for p in range(2):
                here = get(stress, 13 + 9 * p, l, BASE + 8 * t)
                work = get(yface, p, l, 8 * t)
                put(ypart, 4 * p + 3, l, 8 * t, ahead(here) + work - ahead(here + work, -1))
    solid = [flags(8 * t) == 1 for t in range(count)]
    for p in range(2):
        for v in range(5):
            for l in range(2):
                for t in range(count):
                    row = BASE + 8 * t
                    f = SEED + 5 * p + 1 if v == 0 else FLUX + 4 * p + v - 1
                    near = get(bank, f, l, row + 1) - get(bank, f, l, row - 1)
                    far = get(bank, f, l, row + 2) - get(bank, f, l, row - 2)
                    face = get(xface, 5 * p + v, l, row) - get(xface, 5 * p + v, l, row - 1)
                    total = get(acc, 5 * p + v, l, 8 * t) + face - (8.0 / 12.0) * near + (1.0 / 12.0) * far
                    if v > 0:
                        f = 6 + 9 * p + (6 if v == 4 else TENSOR[0][v - 1])
                        viscous = get(stress, f, l, row + 1) - get(stress, f, l, row - 1)
                        viscous = viscous + get(ypart, 4 * p + v - 1, l, 8 * t)
                        wall = get(zface, 4 * p + v - 1, 0, 8 * t)
                        total = total + (viscous + wall if l == 0 else viscous - wall)
                    value = jnp.where(solid[t], -get(bank, SEED + 5 * p + v, l, row), total)
                    emit(5 * p + v, l, 8 * t, value)


def pack_x(flow, colour, flags, weights, to_near, to_far, flow_out, colour_out, flags_out, weights_out, sems):
    pairs = ((flow, flow_out), (colour, colour_out), (flags, flags_out), (weights, weights_out))
    copies = [pltpu.make_async_copy(src, dst, sems.at[i]) for i, (src, dst) in enumerate(pairs)]
    for copy in copies:
        copy.start()
    for copy in copies:
        copy.wait()
    odd = lax.rem(lax.axis_index("gx"), 2)

    def fill(dst, start):
        for l in range(2):
            for v in range(5):
                dst[4 * v + 2 * l : 4 * v + 2 * l + 2, :] = flow_out[v, l, start : start + 2, :]
            dst[20 + 2 * l : 22 + 2 * l, :] = colour_out[l, start : start + 2, :].astype(jnp.float32)

    @pl.when(odd == 0)
    def _():
        fill(to_near, 14)
        fill(to_far, 0)

    @pl.when(odd == 1)
    def _():
        fill(to_near, 0)
        fill(to_far, 14)


def own_cells(flow, colour, weights, bank, acc, table, speed_yz, flux_yz, cell, face):
    for p in range(2):
        for v in range(5):
            line = weights[v, p : p + 1, :]
            table[5 * p + v : 5 * p + v + 1, :] = jnp.concatenate([line, jnp.zeros((1, 101), jnp.float32)], axis=1)
    for l in range(2):
        for c in range(4):
            lanes = slice(128 * c, 128 * c + 128)
            for v in range(5):
                bank[STATE + v, l, c, BASE : BASE + 16, :] = flow[v, l, :, lanes]
            bank[STATE + 5, l, c, BASE : BASE + 16, :] = colour[l, :, lanes].astype(jnp.float32)
    pointwise(bank, table, (BASE, BASE + 8), 8, speed_yz, flux_yz)
    inviscid_yz(bank, speed_yz, flux_yz, cell, face, acc)


def x_halo(near, far, store):
    odd = lax.rem(lax.axis_index("gx"), 2)

    low = jnp.where(odd == 0, far[...], near[...])
    high = jnp.where(odd == 0, near[...], far[...])
    for src, row in ((low, BASE - 2), (high, BASE + 16)):
        for l in range(2):
            for v in range(6):
                store(v, l, row, src, 4 * v + 2 * l)


def fold(first, last):
    rows = first.shape[0] - 8
    lane = lax.broadcasted_iota(jnp.int32, first.shape, 1)
    made = jnp.where(lane < 64, pltpu.roll(first, 32, 1), last)
    return jnp.where((lane[:rows] >= 48) & (lane[:rows] < 112), pltpu.roll(made[8:], 64, 1), made[:rows])


def pack_y(flow, colour, near, far, table, strip, to_far, to_near, edge):
    for l in range(2):
        for side in range(2):
            lanes = slice(384 * side, 384 * side + 128)
            for v in range(5):
                edge[v, l, side, BASE : BASE + 16, :] = flow[v, l, :, lanes]
            edge[5, l, side, BASE : BASE + 16, :] = colour[l, :, lanes].astype(jnp.float32)

    def store(v, l, row, src, at):
        for side in range(2):
            edge[v, l, side, row : row + 2, :] = src[at : at + 2, 384 * side : 384 * side + 128]

    x_halo(near, far, store)
    for v in range(6):
        for l in range(2):
            span = slice(BASE - 4, BASE + 20)
            strip[v, l] = fold(edge[v, l, 0, span, :], edge[v, l, 1, span, :])
    lane = lax.broadcasted_iota(jnp.int32, (16, 128), 1) & 63

    def columns(first):
        made = jnp.zeros((16, 128), jnp.float32)
        for l in range(2):
            for v in range(6):
                at = 2 * (6 * l + v)
                moved = pltpu.roll(strip[v, l], (at - first) % 128, 1)
                made = jnp.where((lane >= at) & (lane < at + 2), moved, made)
        return made

    left, right = columns(32), columns(126)
    odd = lax.rem(lax.axis_index("gy"), 2)

    to_near[...] = jnp.where(odd == 0, right, left)
    to_far[...] = jnp.where(odd == 0, left, right)


def whole_rows(near, far, table, flags, bank_in, acc, bank, result, stress, xface, yface, ypart, zface):
    def store(v, l, row, src, at):
        for c in range(4):
            bank[STATE + v, l, c, row : row + 2, :] = src[at : at + 2, 128 * c : 128 * c + 128]

    x_halo(near, far, store)
    pointwise(bank, table, (BASE - 4, BASE + 12), 8)
    rows = (BASE - 4, BASE + 4, BASE + 12)
    stresses(bank, stress, rows)
    x_faces(bank, stress, xface, rows)
    solid = lambda row: flags[row : row + 8, :]
    emit = lambda f, l, row, value: put(result, f, l, row, value)
    finish(bank, stress, xface, yface, ypart, zface, acc, solid, emit)


def edge_columns(
    far, near, strip, table, flags, result, out, bank, acc, speed_yz, flux_yz, cell, face, stress, xface, yface, ypart,
    zface, staged, middle_sem, edge_sem,
):
    middle = []
    for c in (1, 2):
        lanes = slice(128 * c, 128 * c + 128)
        middle.append(pltpu.make_async_copy(result.at[:, :, c], out.at[:, :, :, lanes], middle_sem.at[c - 1]))
        middle[-1].start()
    lane = lax.broadcasted_iota(jnp.int32, (16, 128), 1)
    place = lane & 63
    odd = lax.rem(lax.axis_index("gy"), 2)

    low = jnp.where(odd == 0, far[...], near[...])
    high = jnp.where(odd == 0, near[...], far[...])
    for l in range(2):
        for v in range(6):
            at = 2 * (6 * l + v)
            made = jnp.where(place < 2, pltpu.roll(high, (-at) % 128, 1), strip[v, l])
            made = jnp.where((place == 30) | (place == 31), pltpu.roll(low, 30 - at, 1), made)
            bank[STATE + v, l, 0, BASE - 4 : BASE + 12, :] = made

    pointwise(bank, table, (BASE - 4,), 16, speed_yz, flux_yz)
    inviscid_yz(bank, speed_yz, flux_yz, cell, face, acc)
    stresses(bank, stress, (BASE - 4,), 16)
    x_faces(bank, stress, xface, (BASE - 4,), 16)
    column = lane[:8]
    solid = lambda row: fold(flags[:, 0:128], flags[:, 384:512])
    copies = []

    def emit(f, l, row, made):
        top, low = slice(0, 8), slice(8, 16)
        half, rest = pltpu.roll(made, 64, 1), pltpu.roll(made, 32, 1)
        staged[0, f, l, top, :] = jnp.where(column < 2, pltpu.roll(made, 96, 1), result[f, l, 0, top, :])
        staged[0, f, l, low, :] = jnp.where(column < 2, rest, result[f, l, 0, low, :])
        staged[1, f, l, top, :] = jnp.where(column >= 126, made, result[f, l, 3, top, :])
        staged[1, f, l, low, :] = jnp.where(column >= 126, half, result[f, l, 3, low, :])
        if l == 1:
            for side in range(2):
                lanes = slice(384 * side, 384 * side + 128)
                copies.append(pltpu.make_async_copy(staged.at[side, f], out.at[f, :, :, lanes], edge_sem.at[side, f]))
                copies[-1].start()

    finish(bank, stress, xface, yface, ypart, zface, acc, solid, emit)
    for copy in middle + copies:
        copy.wait()


def swap(value, axis, offset):
    count = lax.axis_size(axis)
    pairs = []
    for k in range(0, count, 2):
        i, j = (k + offset) % count, (k + offset + 1) % count
        pairs += [(i, j), (j, i)]
    return lax.ppermute(value, axis, pairs)


def local(flow_state, colour_map, cell_flags, probe_weights):
    f32 = jnp.float32
    vmem = pl.BlockSpec(memory_space=pltpu.VMEM)
    hbm = pl.BlockSpec(memory_space=pltpu.HBM)

    def call(kernel, ins, outs, scratch=(), alias={}, cost=0):
        return pl.pallas_call(
            kernel,
            out_shape=[jax.ShapeDtypeStruct(s, d) for s, d, _ in outs],
            in_specs=ins,
            out_specs=[m for _, _, m in outs],
            scratch_shapes=scratch,
            input_output_aliases=alias,
            compiler_params=pltpu.CompilerParams(vmem_limit_bytes=24 * 1024 * 1024),
            cost_estimate=pl.CostEstimate(flops=cost, bytes_accessed=cost, transcendentals=0),
        )

    def banks(n, tiles, rows=ROWS):
        return pltpu.VMEM((n, 2, tiles, rows, 128), f32)

    inputs = [flow_state, colour_map, cell_flags, jnp.transpose(probe_weights, (2, 0, 1))]
    x_near, x_far, flow, colour, flags, weights = call(
        pack_x,
        [hbm] * 4,
        [((24, 512), f32, vmem)] * 2 + [(x.shape, x.dtype, vmem) for x in inputs],
        [pltpu.SemaphoreType.DMA((4,))],
    )(*[pltpu.with_memory_space_constraint(x, pltpu.HBM) for x in inputs])
    x_far = swap(x_far, "gx", 1)
    x_near = swap(x_near, "gx", 0)
    bank, acc, table = call(
        own_cells,
        [vmem] * 3,
        [((FIELDS, 2, 4, ROWS, 128), f32, vmem), ((10, 2, 4, 16, 128), f32, vmem), ((16, 128), f32, vmem)],
        [banks(6, 4), banks(16, 4), banks(10, 4, 16), banks(10, 4, 16)],
        cost=8000000,
    )(flow, colour, weights)
    strip, y_far, y_near = call(
        pack_y,
        [vmem] * 5,
        [((6, 2, 16, 128), f32, vmem), ((16, 128), f32, vmem), ((16, 128), f32, vmem)],
        [banks(6, 2)],
    )(flow, colour, x_near, x_far, table)
    y_far = swap(y_far, "gy", 1)
    y_near = swap(y_near, "gy", 0)
    bank, result = call(
        whole_rows,
        [vmem] * 6,
        [(bank.shape, f32, vmem), (acc.shape, f32, vmem)],
        [banks(24, 4), banks(10, 4), banks(2, 4, 16), banks(8, 4, 16), pltpu.VMEM((8, 1, 4, 16, 128), f32)],
        alias={4: 0, 5: 1},
        cost=8000000,
    )(x_near, x_far, table, flags, bank, acc)
    (out,) = call(
        edge_columns,
        [vmem] * 6,
        [((10, 2, 16, 512), f32, hbm)],
        [
            banks(FIELDS, 1),
            banks(10, 1, 8),
            banks(6, 1),
            banks(16, 1),
            banks(10, 1, 8),
            banks(10, 1, 8),
            banks(24, 1),
            banks(10, 1),
            banks(2, 1, 8),
            banks(8, 1, 8),
            pltpu.VMEM((8, 1, 1, 8, 128), f32),
            pltpu.VMEM((2, 10, 2, 16, 128), f32),
            pltpu.SemaphoreType.DMA((2,)),
            pltpu.SemaphoreType.DMA((2, 10)),
        ],
    )(y_far, y_near, strip, table, flags, result)
    return out.reshape(2, 5, 2, 16, 512)


def solution(mesh):
    return jax.shard_map(
        local,
        mesh=mesh,
        in_specs=(P(None, None, "gx", "gy"), P(None, "gx", "gy"), P("gx", "gy"), P()),
        out_specs=P(None, None, None, "gx", "gy"),
        check_vma=False,
    )
```

```python
import jax
import jax.numpy as jnp
from jax import lax
from jax.experimental import pallas as pl
from jax.experimental.pallas import tpu as pltpu
from jax.sharding import PartitionSpec as P

MU = 0.2
KAPPA = 0.2 * 1.4 / (0.4 * 0.72)
BASE = 12
ROWS = 40
STATE, SEED, PRIM, SPEED, FLUX, FIELDS = 0, 6, 16, 28, 31, 39
TENSOR = ((0, 1, 2), (1, 3, 4), (2, 4, 5))


def get(ref, f, l, row, height=8):
    tiles = [ref[f, l, c, row : row + height, :] for c in range(ref.shape[2])]
    return tiles[0] if len(tiles) == 1 else jnp.concatenate(tiles, axis=1)


def put(ref, f, l, row, value):
    for c in range(ref.shape[2]):
        ref[f, l, c, row : row + value.shape[0], :] = value[:, 128 * c : 128 * c + 128]


def ahead(value, step=1):
    return pltpu.roll(value, (-step) % value.shape[1], 1)


def pointwise(bank, table, rows, height, speed_yz=None, flux_yz=None):
    for l in range(2):
        for row in rows:
            for c in range(bank.shape[2]):
                at = (l, c, slice(row, row + height), slice(None))
                u = [bank[(STATE + v,) + at] for v in range(5)]
                shade = bank[(STATE + 5,) + at].astype(jnp.int32) & 127
                r = 1.0 / u[0]
                vel = [u[1 + e] * r for e in range(3)]
                half = 0.5 * (vel[0] * vel[0] + vel[1] * vel[1] + vel[2] * vel[2])
                pressure = 0.4 * (u[4] - half * u[0])
                heat = pressure * r
                total = u[4] + pressure
                for e in range(3):
                    bank[(PRIM + e,) + at] = vel[e]
                bank[(PRIM + 3,) + at] = heat
                axes = range(1 if flux_yz is None else 3)
                inverse = []
                for e in axes:
                    square = vel[e] * vel[e] + 1.4 * heat
                    inv = lax.rsqrt(square)
                    if e == 0:
                        bank[(SPEED,) + at] = 0.25 * (square * inv)
                    else:
                        speed_yz[(3 * e - 3,) + at] = 0.25 * (square * inv)
                    inverse.append(0.25 * inv)
                for p in range(2):
                    d = []
                    for v in range(5):
                        line = jnp.broadcast_to(table[5 * p + v : 5 * p + v + 1, :], (height, 128))
                        d.append(jnp.take_along_axis(line, shade, axis=1, mode="promise_in_bounds"))
                        bank[(SEED + 5 * p + v,) + at] = d[v]
                    dvel = [(d[1 + e] - vel[e] * d[0]) * r for e in range(3)]
                    dpress = 0.4 * (d[4] - (vel[0] * d[1] + vel[1] * d[2] + vel[2] * d[3]) + half * d[0])
                    dheat = (dpress - heat * d[0]) * r
                    for e in range(3):
                        bank[(PRIM + 4 + 4 * p + e,) + at] = dvel[e]
                    bank[(PRIM + 7 + 4 * p,) + at] = dheat
                    warm = 0.7 * dheat
                    dtotal = d[4] + dpress
                    for e in axes:
                        dspeed = (vel[e] * dvel[e] + warm) * inverse[e]
                        fluxes = []
                        for g in range(3):
                            move = d[1 + g] * vel[e] + u[1 + g] * dvel[e]
                            fluxes.append(move + dpress if g == e else move)
                        fluxes.append(dtotal * vel[e] + total * dvel[e])
                        if e == 0:
                            bank[(SPEED + 1 + p,) + at] = dspeed
                        else:
                            speed_yz[(3 * e - 2 + p,) + at] = dspeed
                        for g in range(4):
                            if e == 0:
                                bank[(FLUX + 4 * p + g,) + at] = fluxes[g]
                            else:
                                flux_yz[(8 * e - 8 + 4 * p + g,) + at] = fluxes[g]


def inviscid_yz(bank, speed_yz, flux_yz, cell, face, acc):
    count = acc.shape[3] // 8
    places = [(l, t) for l in range(2) for t in range(count)]
    for l, t in places:
        row = BASE + 8 * t
        for p in range(2):
            for v in range(5):
                if v == 0:
                    f = get(bank, SEED + 5 * p + 2, l, row)
                else:
                    f = get(flux_yz, 4 * p + v - 1, l, row)
                put(cell, 5 * p + v, l, 8 * t, (8.0 / 12.0) * f - (1.0 / 12.0) * (ahead(f) + ahead(f, -1)))
    for l, t in places:
        row = BASE + 8 * t
        here = get(speed_yz, 0, l, row)
        s_sum = here + ahead(here)
        ds = []
        for p in range(2):
            here = get(speed_yz, 1 + p, l, row)
            ds.append(here + ahead(here))
        for v in range(5):
            here = get(bank, STATE + v, l, row)
            jump = ahead(here) - here
            for p in range(2):
                here = get(bank, SEED + 5 * p + v, l, row)
                central = get(cell, 5 * p + v, l, 8 * t)
                made = ds[p] * jump + s_sum * (ahead(here) - here) - (central + ahead(central))
                put(face, 5 * p + v, l, 8 * t, made)
    for t in range(count):
        row = BASE + 8 * t
        s_sum = get(speed_yz, 3, 0, row) + get(speed_yz, 3, 1, row)
        ds = [get(speed_yz, 4 + p, 0, row) + get(speed_yz, 4 + p, 1, row) for p in range(2)]
        for v in range(5):
            jump = get(bank, STATE + v, 1, row) - get(bank, STATE + v, 0, row)
            for p in range(2):
                if v == 0:
                    mean = get(bank, SEED + 5 * p + 3, 0, row) + get(bank, SEED + 5 * p + 3, 1, row)
                else:
                    mean = get(flux_yz, 8 + 4 * p + v - 1, 0, row) + get(flux_yz, 8 + 4 * p + v - 1, 1, row)
                djump = get(bank, SEED + 5 * p + v, 1, row) - get(bank, SEED + 5 * p + v, 0, row)
                wall = 0.5 * mean - (ds[p] * jump + s_sum * djump)
                for l in range(2):
                    made = get(face, 5 * p + v, l, 8 * t)
                    made = made - ahead(made, -1)
                    put(acc, 5 * p + v, l, 8 * t, made + wall if l == 1 else made - wall)


def stresses(bank, stress, rows, height=8):
    quarter = 0.25 * MU
    for row in rows:
        for k in range(3):
            q = PRIM + 4 * k
            grad_z = [2.0 * (get(bank, q + i, 1, row, height) - get(bank, q + i, 0, row, height)) for i in range(4 if k else 3)]
            for l in range(2):
                count = range(4 if k else 3)
                grad_x = [get(bank, q + i, l, row + 1, height) - get(bank, q + i, l, row - 1, height) for i in count]
                here = [get(bank, q + i, l, row, height) for i in count]
                grad_y = [ahead(h, 1) - ahead(h, -1) for h in here]
                third = (2.0 / 3.0) * (grad_x[0] + grad_y[1] + grad_z[2])
                base = 9 * k - 3 if k else 0
                put(stress, base, l, row, quarter * (2.0 * grad_x[0] - third))
                put(stress, base + 1, l, row, quarter * (grad_y[0] + grad_x[1]))
                put(stress, base + 2, l, row, quarter * (grad_z[0] + grad_x[2]))
                put(stress, base + 3, l, row, quarter * (2.0 * grad_y[1] - third))
                put(stress, base + 4, l, row, quarter * (grad_z[1] + grad_y[2]))
                put(stress, base + 5, l, row, quarter * (2.0 * grad_z[2] - third))
                if k > 0:
                    put(stress, base + 6, l, row, (0.25 * KAPPA) * grad_x[3])
                    put(stress, base + 7, l, row, (0.25 * KAPPA) * grad_y[3])
                    put(stress, base + 8, l, row, (0.25 * KAPPA) * grad_z[3])


def x_faces(bank, stress, xface, rows, height=8):
    for l in range(2):
        for row in rows:
            pair = lambda ref, f: get(ref, f, l, row, height) + get(ref, f, l, row + 1, height)
            s_sum = pair(bank, SPEED)
            ds = [pair(bank, SPEED + 1 + p) for p in range(2)]
            for v in range(5):
                jump = get(bank, STATE + v, l, row + 1, height) - get(bank, STATE + v, l, row, height)
                for p in range(2):
                    f = SEED + 5 * p + v
                    made = ds[p] * jump + s_sum * (get(bank, f, l, row + 1, height) - get(bank, f, l, row, height))
                    if v == 4:
                        work = 0.0
                        for e in range(3):
                            i = TENSOR[0][e]
                            work = work + pair(bank, PRIM + e) * pair(stress, 6 + 9 * p + i)
                            work = work + pair(bank, PRIM + 4 + 4 * p + e) * pair(stress, i)
                        made = made + 0.5 * work
                    put(xface, 5 * p + v, l, row, made)


def finish(bank, stress, xface, yface, ypart, zface, acc, flags, emit):
    count = acc.shape[3] // 8
    for t in range(count):
        row = BASE + 8 * t
        for l in range(2):
            def pair(ref, f):
                here = get(ref, f, l, row)
                return here + ahead(here)

            v_sum = [pair(bank, PRIM + e) for e in range(3)]
            t_sum = [pair(stress, i) for i in TENSOR[1]]
            for p in range(2):
                work = 0.0
                for e in range(3):
                    here = get(stress, 6 + 9 * p + TENSOR[1][e], l, row)
                    after = ahead(here)
                    put(ypart, 4 * p + e, l, 8 * t, after - ahead(here, -1))
                    work = work + v_sum[e] * (here + after)
                    work = work + pair(bank, PRIM + 4 + 4 * p + e) * t_sum[e]
                put(yface, p, l, 8 * t, 0.5 * work)
        both = lambda ref, f: get(ref, f, 0, row) + get(ref, f, 1, row)
        v_sum = [both(bank, PRIM + e) for e in range(3)]
        t_sum = [both(stress, i) for i in TENSOR[2]]
        for p in range(2):
            work = 0.0
            for e in range(3):
                dt = both(stress, 6 + 9 * p + TENSOR[2][e])
                put(zface, 4 * p + e, 0, 8 * t, dt)
                work = work + v_sum[e] * dt + both(bank, PRIM + 4 + 4 * p + e) * t_sum[e]
            put(zface, 4 * p + 3, 0, 8 * t, 0.5 * work + both(stress, 6 + 9 * p + 8))
    for t in range(count):
        for l in range(2):
            for p in range(2):
                here = get(stress, 13 + 9 * p, l, BASE + 8 * t)
                work = get(yface, p, l, 8 * t)
                put(ypart, 4 * p + 3, l, 8 * t, ahead(here) + work - ahead(here + work, -1))
    solid = [flags(8 * t) == 1 for t in range(count)]
    for p in range(2):
        for v in range(5):
            for l in range(2):
                for t in range(count):
                    row = BASE + 8 * t
                    f = SEED + 5 * p + 1 if v == 0 else FLUX + 4 * p + v - 1
                    near = get(bank, f, l, row + 1) - get(bank, f, l, row - 1)
                    far = get(bank, f, l, row + 2) - get(bank, f, l, row - 2)
                    face = get(xface, 5 * p + v, l, row) - get(xface, 5 * p + v, l, row - 1)
                    total = get(acc, 5 * p + v, l, 8 * t) + face - (8.0 / 12.0) * near + (1.0 / 12.0) * far
                    if v > 0:
                        f = 6 + 9 * p + (6 if v == 4 else TENSOR[0][v - 1])
                        viscous = get(stress, f, l, row + 1) - get(stress, f, l, row - 1)
                        viscous = viscous + get(ypart, 4 * p + v - 1, l, 8 * t)
                        wall = get(zface, 4 * p + v - 1, 0, 8 * t)
                        total = total + (viscous + wall if l == 0 else viscous - wall)
                    value = jnp.where(solid[t], -get(bank, SEED + 5 * p + v, l, row), total)
                    emit(5 * p + v, l, 8 * t, value)


def pack_x(flow, colour, flags, weights, to_near, to_far, flow_out, colour_out, flags_out, weights_out, sems):
    pairs = ((flow, flow_out), (colour, colour_out), (flags, flags_out), (weights, weights_out))
    copies = [pltpu.make_async_copy(src, dst, sems.at[i]) for i, (src, dst) in enumerate(pairs)]
    for copy in copies:
        copy.start()
    for copy in copies:
        copy.wait()
    odd = lax.rem(lax.axis_index("gx"), 2)

    def fill(dst, start):
        for l in range(2):
            for v in range(5):
                dst[4 * v + 2 * l : 4 * v + 2 * l + 2, :] = flow_out[v, l, start : start + 2, :]
            dst[20 + 2 * l : 22 + 2 * l, :] = colour_out[l, start : start + 2, :].astype(jnp.float32)

    @pl.when(odd == 0)
    def _():
        fill(to_near, 14)
        fill(to_far, 0)

    @pl.when(odd == 1)
    def _():
        fill(to_near, 0)
        fill(to_far, 14)


def own_cells(flow, colour, weights, bank, acc, table, speed_yz, flux_yz, cell, face):
    for p in range(2):
        for v in range(5):
            line = weights[v, p : p + 1, :]
            table[5 * p + v : 5 * p + v + 1, :] = jnp.concatenate([line, jnp.zeros((1, 101), jnp.float32)], axis=1)
    for l in range(2):
        for c in range(4):
            lanes = slice(128 * c, 128 * c + 128)
            for v in range(5):
                bank[STATE + v, l, c, BASE : BASE + 16, :] = flow[v, l, :, lanes]
            bank[STATE + 5, l, c, BASE : BASE + 16, :] = colour[l, :, lanes].astype(jnp.float32)
    pointwise(bank, table, (BASE, BASE + 8), 8, speed_yz, flux_yz)
    inviscid_yz(bank, speed_yz, flux_yz, cell, face, acc)


def x_halo(near, far, store):
    odd = lax.rem(lax.axis_index("gx"), 2)

    low = jnp.where(odd == 0, far[...], near[...])
    high = jnp.where(odd == 0, near[...], far[...])
    for src, row in ((low, BASE - 2), (high, BASE + 16)):
        for l in range(2):
            for v in range(6):
                store(v, l, row, src, 4 * v + 2 * l)


def fold(first, last):
    rows = first.shape[0] - 8
    lane = lax.broadcasted_iota(jnp.int32, first.shape, 1)
    made = jnp.where(lane < 64, pltpu.roll(first, 32, 1), last)
    return jnp.where((lane[:rows] >= 48) & (lane[:rows] < 112), pltpu.roll(made[8:], 64, 1), made[:rows])


def pack_y(flow, colour, near, far, table, strip, to_near, to_far, edge):
    for l in range(2):
        for side in range(2):
            lanes = slice(384 * side, 384 * side + 128)
            for v in range(5):
                edge[v, l, side, BASE : BASE + 16, :] = flow[v, l, :, lanes]
            edge[5, l, side, BASE : BASE + 16, :] = colour[l, :, lanes].astype(jnp.float32)

    def store(v, l, row, src, at):
        for side in range(2):
            edge[v, l, side, row : row + 2, :] = src[at : at + 2, 384 * side : 384 * side + 128]

    x_halo(near, far, store)
    for v in range(6):
        for l in range(2):
            span = slice(BASE - 4, BASE + 20)
            strip[v, l] = fold(edge[v, l, 0, span, :], edge[v, l, 1, span, :])
    lane = lax.broadcasted_iota(jnp.int32, (16, 128), 1) & 63

    def columns(first):
        made = jnp.zeros((16, 128), jnp.float32)
        for l in range(2):
            for v in range(6):
                at = 2 * (6 * l + v)
                moved = pltpu.roll(strip[v, l], (at - first) % 128, 1)
                made = jnp.where((lane >= at) & (lane < at + 2), moved, made)
        return made

    left, right = columns(32), columns(126)
    odd = lax.rem(lax.axis_index("gy"), 2)

    to_near[...] = jnp.where(odd == 0, right, left)
    to_far[...] = jnp.where(odd == 0, left, right)


def whole_rows(near, far, table, flags, bank_in, acc, bank, result, stress, xface, yface, ypart, zface):
    def store(v, l, row, src, at):
        for c in range(4):
            bank[STATE + v, l, c, row : row + 2, :] = src[at : at + 2, 128 * c : 128 * c + 128]

    x_halo(near, far, store)
    pointwise(bank, table, (BASE - 4, BASE + 12), 8)
    rows = (BASE - 4, BASE + 4, BASE + 12)
    stresses(bank, stress, rows)
    x_faces(bank, stress, xface, rows)
    solid = lambda row: flags[row : row + 8, :]
    emit = lambda f, l, row, value: put(result, f, l, row, value)
    finish(bank, stress, xface, yface, ypart, zface, acc, solid, emit)


def edge_columns(
    near, far, strip, table, flags, result, out, bank, acc, speed_yz, flux_yz, cell, face, stress, xface, yface, ypart,
    zface, staged, middle_sem, edge_sem,
):
    middle = []
    for c in (1, 2):
        lanes = slice(128 * c, 128 * c + 128)
        middle.append(pltpu.make_async_copy(result.at[:, :, c], out.at[:, :, :, lanes], middle_sem.at[c - 1]))
        middle[-1].start()
    lane = lax.broadcasted_iota(jnp.int32, (16, 128), 1)
    place = lane & 63
    odd = lax.rem(lax.axis_index("gy"), 2)

    low = jnp.where(odd == 0, far[...], near[...])
    high = jnp.where(odd == 0, near[...], far[...])
    for l in range(2):
        for v in range(6):
            at = 2 * (6 * l + v)
            made = jnp.where(place < 2, pltpu.roll(high, (-at) % 128, 1), strip[v, l])
            made = jnp.where((place == 30) | (place == 31), pltpu.roll(low, 30 - at, 1), made)
            bank[STATE + v, l, 0, BASE - 4 : BASE + 12, :] = made

    pointwise(bank, table, (BASE - 4,), 16, speed_yz, flux_yz)
    inviscid_yz(bank, speed_yz, flux_yz, cell, face, acc)
    stresses(bank, stress, (BASE - 4,), 16)
    x_faces(bank, stress, xface, (BASE - 4,), 16)
    column = lane[:8]
    solid = lambda row: fold(flags[:, 0:128], flags[:, 384:512])
    copies = []

    def emit(f, l, row, made):
        top, low = slice(0, 8), slice(8, 16)
        half, rest = pltpu.roll(made, 64, 1), pltpu.roll(made, 32, 1)
        staged[0, f, l, top, :] = jnp.where(column < 2, pltpu.roll(made, 96, 1), result[f, l, 0, top, :])
        staged[0, f, l, low, :] = jnp.where(column < 2, rest, result[f, l, 0, low, :])
        staged[1, f, l, top, :] = jnp.where(column >= 126, made, result[f, l, 3, top, :])
        staged[1, f, l, low, :] = jnp.where(column >= 126, half, result[f, l, 3, low, :])
        if l == 1:
            for side in range(2):
                lanes = slice(384 * side, 384 * side + 128)
                copies.append(pltpu.make_async_copy(staged.at[side, f], out.at[f, :, :, lanes], edge_sem.at[side, f]))
                copies[-1].start()

    finish(bank, stress, xface, yface, ypart, zface, acc, solid, emit)
    for copy in middle + copies:
        copy.wait()


def swap(value, axis, offset):
    count = lax.axis_size(axis)
    pairs = []
    for k in range(0, count, 2):
        i, j = (k + offset) % count, (k + offset + 1) % count
        pairs += [(i, j), (j, i)]
    return lax.ppermute(value, axis, pairs)


def local(flow_state, colour_map, cell_flags, probe_weights):
    f32 = jnp.float32
    vmem = pl.BlockSpec(memory_space=pltpu.VMEM)
    hbm = pl.BlockSpec(memory_space=pltpu.HBM)

    def call(kernel, ins, outs, scratch=(), alias={}, cost=0):
        return pl.pallas_call(
            kernel,
            out_shape=[jax.ShapeDtypeStruct(s, d) for s, d, _ in outs],
            in_specs=ins,
            out_specs=[m for _, _, m in outs],
            scratch_shapes=scratch,
            input_output_aliases=alias,
            compiler_params=pltpu.CompilerParams(vmem_limit_bytes=24 * 1024 * 1024),
            cost_estimate=pl.CostEstimate(flops=cost, bytes_accessed=cost, transcendentals=0),
        )

    def banks(n, tiles, rows=ROWS):
        return pltpu.VMEM((n, 2, tiles, rows, 128), f32)

    inputs = [flow_state, colour_map, cell_flags, jnp.transpose(probe_weights, (2, 0, 1))]
    x_near, x_far, flow, colour, flags, weights = call(
        pack_x,
        [hbm] * 4,
        [((24, 512), f32, vmem)] * 2 + [(x.shape, x.dtype, vmem) for x in inputs],
        [pltpu.SemaphoreType.DMA((4,))],
    )(*[pltpu.with_memory_space_constraint(x, pltpu.HBM) for x in inputs])
    x_far = swap(x_far, "gx", 1)
    x_near = swap(x_near, "gx", 0)
    bank, acc, table = call(
        own_cells,
        [vmem] * 3,
        [((FIELDS, 2, 4, ROWS, 128), f32, vmem), ((10, 2, 4, 16, 128), f32, vmem), ((16, 128), f32, vmem)],
        [banks(6, 4), banks(16, 4), banks(10, 4, 16), banks(10, 4, 16)],
        cost=8000000,
    )(flow, colour, weights)
    strip, y_near, y_far = call(
        pack_y,
        [vmem] * 5,
        [((6, 2, 16, 128), f32, vmem), ((16, 128), f32, vmem), ((16, 128), f32, vmem)],
        [banks(6, 2)],
    )(flow, colour, x_near, x_far, table)
    y_far = swap(y_far, "gy", 1)
    y_near = swap(y_near, "gy", 0)
    bank, result = call(
        whole_rows,
        [vmem] * 6,
        [(bank.shape, f32, vmem), (acc.shape, f32, vmem)],
        [banks(24, 4), banks(10, 4), banks(2, 4, 16), banks(8, 4, 16), pltpu.VMEM((8, 1, 4, 16, 128), f32)],
        alias={4: 0, 5: 1},
        cost=8000000,
    )(x_near, x_far, table, flags, bank, acc)
    (out,) = call(
        edge_columns,
        [vmem] * 6,
        [((10, 2, 16, 512), f32, hbm)],
        [
            banks(FIELDS, 1),
            banks(10, 1, 8),
            banks(6, 1),
            banks(16, 1),
            banks(10, 1, 8),
            banks(10, 1, 8),
            banks(24, 1),
            banks(10, 1),
            banks(2, 1, 8),
            banks(8, 1, 8),
            pltpu.VMEM((8, 1, 1, 8, 128), f32),
            pltpu.VMEM((2, 10, 2, 16, 128), f32),
            pltpu.SemaphoreType.DMA((2,)),
            pltpu.SemaphoreType.DMA((2, 10)),
        ],
    )(y_near, y_far, strip, table, flags, result)
    return out.reshape(2, 5, 2, 16, 512)


def solution(mesh):
    return jax.shard_map(
        local,
        mesh=mesh,
        in_specs=(P(None, None, "gx", "gy"), P(None, "gx", "gy"), P("gx", "gy"), P()),
        out_specs=P(None, None, None, "gx", "gy"),
        check_vma=False,
    )
```
